512 devices in a mesh: fsdp: 128 (over y_lo, x, z, core), tp: 4 (over y_hi).
Axes of the slice: x: 4, y: 8 (y_hi: 4, y_lo: 2; y = y_hi * 2 + y_lo), z: 8, core: 2. Of those that a mesh axis runs over, the one named last changes fastest.
Arguments:
- token_grads: float32 [32768, 128], P('fsdp'), may hold values from -96 to 96
- hidden: bfloat16 [32768, 2048], P('fsdp', 'tp')
- proj_weight: float32 [128, 2048], P(None, 'tp'), may hold values from -0.125 to 0.125
- proj_bias: float32 [128], replicated, may hold values from -4 to 4
- norm_gain: float32 [2048], P('tp'), may hold values from 0.1 to 1.9
- down_weight: float32 [5632, 2048], P('tp', 'fsdp'), may hold values from -0.5 to 0.5
- lengths: int32 [64], replicated, may hold values from 1 to 512, as said below
Outputs:
- act_grad: bfloat16 [32768, 5632], P('fsdp', 'tp')
- proj_grad: float32 [128, 2048], P(None, 'tp')
- gain_grad: float32 [2048], P('tp')
- bias_grad: float32 [128], replicated
The draws below stay inside these ranges and needn't reach their ends.
Inputs may be any that keep to these rules, and one draw needn't show every extreme that they name: `lengths`: every sequence has at least one valid token, and some sequence is full.
All inputs are finite; a program needn't handle non-finite values.
Results may differ from the reference program's by a relative error of at most 0.018.
Values may be sent and summed in bfloat16 or wider, within the bound.
A program may use at most 64 MiB of HBM per device.

```python
import math
import jax
import jax.numpy as jnp
from jax import lax

D = 2048
HID = 5632
E = 128
LEN = 512
TOK_DEV = 256
TOKENS = 32768
SEQS = 64
N_FSDP = 128


def draw_hidden(key, part):
    key = jax.random.fold_in(key, 11)
    first, second, third = jax.random.split(key, 3)
    base = jax.random.normal(first, (TOKENS, D), jnp.float32)
    row_scale = jnp.exp(jax.random.uniform(second, (TOKENS, 1), jnp.float32) * math.log(10.0)) / 3.0
    col_scale = jnp.exp(jax.random.uniform(third, (1, D), jnp.float32) * math.log(4.0)) / 2.0
    return (base * row_scale * col_scale).astype(jnp.bfloat16)


def draw_lengths(key, part):
    key = jax.random.fold_in(key, 23)
    first, second = jax.random.split(key)
    values = jax.random.randint(first, (SEQS,), 1, LEN + 1)
    chosen = jax.random.randint(second, (), 0, SEQS)
    return jnp.where(jnp.arange(SEQS) == chosen, LEN, values).astype(jnp.int32)


def block_scale(own_key, dims, shards, smallest, high):
    def one(axis_at, shards_of):
        draws = jax.random.uniform(jax.random.fold_in(jax.random.fold_in(own_key, 6), axis_at), (shards_of,), jnp.float32, smallest / len(shards), high / len(shards))
        return jnp.repeat(jnp.exp(draws), dims[axis_at] // shards_of).reshape((-1,) + (1,) * (len(dims) - axis_at - 1))

    factor_of = one(*shards[0])
    for cut in shards[1:]:
        factor_of = factor_of * one(*cut)
    return factor_of


def gaussian(stream_key, extent, spread, bound, cuts=(), kind=jnp.bfloat16):
    entries = spread * jax.random.normal(stream_key, extent, jnp.float32)
    if cuts:
        entries = entries * block_scale(stream_key, extent, cuts, -0.22, 0.18)
    return jnp.clip(entries, -bound, bound).astype(kind)


def setup_inputs(seed: int = 0) -> dict:
    arg_keys = jax.random.split(jax.random.key(seed), 8)
    token_grads = gaussian(arg_keys[0], (TOKENS, E), 16.0, 96.0, ((0, 128),), jnp.float32)
    hidden = draw_hidden(jax.random.fold_in(arg_keys[7], 71), 0)
    proj_weight = gaussian(arg_keys[2], (E, D), D ** -0.5, 0.125, ((1, 4),), jnp.float32)
    proj_bias = gaussian(arg_keys[3], (E,), 1.0, 4.0, (), jnp.float32)
    norm_gain = jnp.clip(1.0 + 0.18 * jax.random.normal(arg_keys[4], (D,), jnp.float32), 0.1, 1.9)
    down_weight = gaussian(arg_keys[5], (HID, D), (D // 16) ** -0.5, 0.5, ((0, 4), (1, 128)), jnp.float32)
    lengths = draw_lengths(jax.random.fold_in(arg_keys[7], 71), 0)
    return {"token_grads": token_grads, "hidden": hidden, "proj_weight": proj_weight, "proj_bias": proj_bias, "norm_gain": norm_gain, "down_weight": down_weight, "lengths": lengths}


def reference(token_grads, hidden, proj_weight, proj_bias, norm_gain, down_weight, lengths):
    ordered = token_grads.reshape(N_FSDP, N_FSDP, TOK_DEV // N_FSDP, E)
    ordered = ordered.transpose(1, 0, 2, 3).reshape(N_FSDP, TOK_DEV, E)
    blocks = hidden.reshape(N_FSDP, TOK_DEV, D)
    down_low = down_weight.astype(jnp.bfloat16)
    high = lax.Precision.HIGHEST

    def one_block(carry, item):
        proj_sum, gain_sum, bias_sum = carry
        grads, rows, index = item
        tokens = index * TOK_DEV + jnp.arange(TOK_DEV, dtype=jnp.int32)
        live = tokens % LEN < lengths[tokens // LEN]
        grads = jnp.where(live[:, None], grads, jnp.float32(0.0))
        xvals = rows.astype(jnp.float32)
        inv = lax.rsqrt(lax.optimization_barrier(jnp.sum(xvals * xvals, axis=1)) / D + 1e-06)
        scaled = xvals * norm_gain
        u_proj = jnp.dot(scaled, proj_weight.T, precision=high)
        zvals = inv[:, None] * u_proj + proj_bias
        kinv = lax.rsqrt(lax.optimization_barrier(jnp.sum(zvals * zvals, axis=1)) + 1e-06)
        emb = zvals * kinv[:, None]
        dz = kinv[:, None] * (grads - emb * lax.optimization_barrier(jnp.sum(emb * grads, axis=1))[:, None])
        dn = jnp.dot(dz, proj_weight, precision=high)
        cvals = lax.optimization_barrier(jnp.sum(dz * u_proj, axis=1))
        dh = (inv[:, None] * norm_gain * dn - xvals * (inv ** 3 * cvals / D)[:, None]).astype(jnp.bfloat16)
        act = jnp.dot(dh, down_low.T, preferred_element_type=jnp.float32).astype(jnp.bfloat16)
        normed = scaled * inv[:, None]
        proj_sum = proj_sum + jnp.dot(dz.T, normed, precision=high)
        gain_sum = gain_sum + lax.optimization_barrier(jnp.sum(dn * xvals * inv[:, None], axis=0))
        bias_sum = bias_sum + lax.optimization_barrier(jnp.sum(dz, axis=0))
        return ((proj_sum, gain_sum, bias_sum), act)
    start = (jnp.zeros((E, D), jnp.float32), jnp.zeros((D,), jnp.float32), jnp.zeros((E,), jnp.float32))
    sums, acts = lax.scan(one_block, start, (ordered, blocks, jnp.arange(N_FSDP, dtype=jnp.int32)))
    count = jnp.float32(SEQS)
    return (acts.reshape(TOKENS, HID), sums[0] / count, sums[1] / count, sums[2] / count)
```

```python
import jax
import jax.numpy as jnp
from jax import lax
from jax.experimental import pallas as pl
from jax.experimental.pallas import tpu as pltpu
from jax.sharding import PartitionSpec as P

D = 2048
LEN = 512
NX, NZ, NG, NP, NT = 4, 8, 8, 16, 4
MESH = pl.DeviceIdType.MESH
HIGH = lax.Precision.HIGHEST
BF, F32, I32 = jnp.bfloat16, jnp.float32, jnp.int32
NT_DIMS = (((1,), (1,)), ((), ()))


def iota(shape, axis):
    return lax.broadcasted_iota(I32, shape, axis)


def split_hi_lo(value):
    hi = value.astype(BF).astype(F32)
    return hi, value - hi


def permute_rows(count, source_of, rows):
    hot = jnp.where(
        iota((count, count), 1) == source_of(iota((count, count), 0)), F32(1.0), F32(0.0)
    ).astype(BF)
    return jnp.dot(hot, rows, preferred_element_type=F32)


def kernel(
    tg_ref, x_ref, p_ref, b_ref, g_ref, w_ref, len_ref,
    act_ref, proj_ref, gain_ref, bias_ref,
    wfull, usend, urecv, s1src, s1dst, s2src, s2dst, dzfull, dhfull, rs_src, rs_dst, zbuf, ag,
    a1s, a1r, zs0, zr0, b1s, b1r, zs1, zr1, xs, xr, xfs, xfr, sibs, sibr,
    s1ss, s1rs, s2ss, s2rs, us, ur, ds, dr, dhs, dhr, dfs, dfr, rss, rsr, zss, zsr, ags, agr,
):
    f = lax.axis_index("fsdp")
    t = lax.axis_index("tp")
    core = f % 2
    z = (f // 2) % NZ
    grp = f // 16
    xa = grp % NX
    yl = grp // NX
    p = grp * 2 + core

    def at_f(group, zpos, cpos):
        return group * 16 + zpos * 2 + cpos

    def peer_p(d):
        q = (p + d) % NP
        return q, at_f(q // 2, z, q % 2)

    def peer_z(d):
        q = (z + d) % NZ
        return q, at_f(grp, q, core)

    def peer_t(d):
        return (t + d) % NT

    def copy(src, dst, ssem, rsem, dev):
        return pltpu.make_async_remote_copy(
            src_ref=src, dst_ref=dst, send_sem=ssem, recv_sem=rsem,
            device_id=dev, device_id_type=MESH,
        )

    def each(lo, hi, body):
        def step(d, carry):
            body(d)
            return carry

        lax.fori_loop(lo, hi, step, 0)

    bar = pltpu.get_barrier_semaphore()

    def greet(dev):
        pl.semaphore_signal(bar, inc=1, device_id=dev, device_id_type=MESH)

    each(1, NP, lambda d: greet({"fsdp": peer_p(d)[1]}))
    each(1, NZ, lambda d: greet({"fsdp": peer_z(d)[1]}))
    each(1, NT, lambda d: greet({"tp": peer_t(d)}))

    wfull[yl, xa, z, core] = w_ref[...].astype(BF)
    tg = permute_rows(
        256, lambda r: ((r >> 2) & 7) * 32 + (r >> 5) * 4 + (r & 3), tg_ref[...].astype(BF)
    )
    s1src[...] = tg.astype(BF).reshape(8, 32, 128)
    xv = x_ref[...].astype(F32)
    pu = lax.dot_general(xv * g_ref[...], p_ref[...], NT_DIMS, precision=HIGH)
    sq_hi, sq_lo = split_hi_lo(jnp.sum(xv * xv, axis=1, keepdims=True))
    sq2 = jnp.where(iota((256, 128), 1) < 64, sq_hi, sq_lo)
    usend[:, :, :, 0:128] = pu.astype(BF).reshape(2, 4, 32, 128)
    usend[:, :, :, 128:256] = sq2.astype(BF).reshape(2, 4, 32, 128)
    pl.semaphore_wait(bar, (NP - 1) + (NZ - 1) + (NT - 1))

    sends0, sends1 = [], []

    def go(sends, make):
        make().start()
        sends.append(make)

    def sibling(piece):
        copy(piece, piece, sibs, sibr, {"fsdp": f + 1 - 2 * core}).start()

    own = wfull.at[yl, xa, z, core]
    zdev = ({"fsdp": at_f(grp, (z + 1) % NZ, core)}, {"fsdp": at_f(grp, (z + NZ - 1) % NZ, core)})
    xdev = (
        {"fsdp": at_f(yl * NX + (xa + 1) % NX, z, core)},
        {"fsdp": at_f(yl * NX + (xa + NX - 1) % NX, z, core)},
    )

    def zslot(direction, s):
        return (z + NZ - s) % NZ if direction == 0 else (z + s) % NZ

    def piece0(h, zj):
        return wfull.at[h, :, zj, 0]

    def zmove0(direction, s, h):
        def make():
            piece = piece0(h, zslot(direction, s))
            return copy(piece, piece, zs0.at[direction, s, h], zr0.at[direction, s, h], zdev[direction])

        return make

    def begin0():
        for d in range(1, NG):
            go(sends0, lambda d=d: copy(
                own, own, a1s.at[d], a1r.at[d], {"fsdp": at_f((grp + d) % NG, z, core)}))

    def first0():
        for d in range(1, NG):
            copy(own, own, a1s.at[d], a1r.at[d], zdev[0]).wait_recv()
        for direction, h in ((0, 0), (1, 1), (0, 1), (1, 0)):
            go(sends0, zmove0(direction, 0, h))
        sibling(wfull.at[:, :, z, 0])

    def step0(s, direction, h):
        def run():
            zmove0(direction, s - 1, h)().wait_recv()
            if s < 3 or (s == 3 and h == direction):
                go(sends0, zmove0(direction, s, h))
            sibling(piece0(h, zslot(direction, s)))

        return run

    todo0 = [first0]
    for s in (1, 2, 3):
        todo0 += [step0(s, d, h) for d, h in ((0, 0), (1, 1), (0, 1), (1, 0))]
    todo0 += [step0(4, 0, 0), step0(4, 1, 1)]

    hops = [(0, 0), (0, 1), (1, 1), (0, 2), (1, 2), (0, 3), (1, 3), (0, 4)]

    def piece1(xj, zj):
        return wfull.at[:, xj, zj, 1]

    def zmove1(direction, s):
        def make():
            piece = piece1(xa, zslot(direction, s))
            return copy(piece, piece, zs1.at[direction, s], zr1.at[direction, s], zdev[direction])

        return make

    def xmove(direction, k):
        def make():
            piece = piece1(xa, zslot(*hops[k]))
            return copy(piece, piece, xs.at[direction, k], xr.at[direction, k], xdev[direction])

        return make

    def xforward(k):
        direction = k % 2

        def make():
            xj = (xa + NX - 1) % NX if direction == 0 else (xa + 1) % NX
            piece = piece1(xj, zslot(*hops[k]))
            return copy(piece, piece, xfs.at[k], xfr.at[k], xdev[direction])

        return make

    def begin1():
        go(sends1, lambda: copy(own, own, b1s, b1r, {"fsdp": at_f((grp + NX) % NG, z, core)}))

    def spread(k):
        go(sends1, xmove(0, k))
        go(sends1, xmove(1, k))
        sibling(piece1(xa, zslot(*hops[k])))

    def first1():
        copy(own, own, b1s, b1r, zdev[0]).wait_recv()
        go(sends1, zmove1(0, 0))
        go(sends1, zmove1(1, 0))
        spread(0)

    def zstep1(k):
        def run():
            direction, s = hops[k]
            zmove1(direction, s - 1)().wait_recv()
            if s < 3 or (s == 3 and direction == 0):
                go(sends1, zmove1(direction, s))
            spread(k)

        return run

    def xstep1(k, direction):
        def run():
            xmove(direction, k)().wait_recv()
            xj = (xa + NX - 1) % NX if direction == 0 else (xa + 1) % NX
            if k % 2 == direction:
                go(sends1, xforward(k))
            sibling(piece1(xj, zslot(*hops[k])))

        return run

    def fstep1(k):
        def run():
            xforward(k)().wait_recv()
            sibling(piece1((xa + 2) % NX, zslot(*hops[k])))

        return run

    todo1 = [first1]
    for k in range(1, 8):
        todo1.append(zstep1(k))
        if k >= 3:
            todo1 += [xstep1(k - 3, 0), xstep1(k - 3, 1)]
        if k >= 6:
            todo1.append(fstep1(k - 6))
    for k in (5, 6, 7):
        todo1 += [xstep1(k, 0), xstep1(k, 1), fstep1(k - 3)]
    todo1 += [fstep1(k) for k in (5, 6, 7)]

    def advance(n0, n1):
        head0, head1 = todo0[:n0], todo1[:n1]
        del todo0[:n0], todo1[:n1]
        if head0:
            @pl.when(core == 0)
            def _():
                for run in head0:
                    run()
        if head1:
            @pl.when(core == 1)
            def _():
                for run in head1:
                    run()

    todo0.insert(0, begin0)
    todo1.insert(0, begin1)
    advance(1, 1)

    carries = xa == t

    @pl.when(carries)
    def _():
        def send(d):
            q, dev = peer_z(d)
            copy(s1src.at[q], s1dst.at[z], s1ss.at[d], s1rs.at[d], {"fsdp": dev}).start()

        each(1, NZ, send)
        s1dst[z] = s1src[z]

    def send_u(d):
        q = peer_t(d)
        copy(usend.at[:, q], urecv.at[t], us.at[d], ur.at[d], {"tp": q}).start()

    each(1, NT, send_u)
    urecv[t] = usend[:, t]
    advance(1, 1)

    slot = yl * 2 + core

    @pl.when(carries)
    def _():
        each(1, NZ, lambda d: copy(
            s1src.at[0], s1dst.at[0], s1ss.at[d], s1rs.at[d], {"fsdp": peer_z(d)[1]}).wait_recv())
        rows = permute_rows(
            256,
            lambda r: ((r >> 1) & 7) * 32 + (r >> 4) * 2 + (r & 1),
            s1dst[...].reshape(256, 128),
        )
        s2src[...] = rows.astype(BF).reshape(16, 16, 128)

        def send(d):
            q, dev = peer_p(d)
            copy(s2src.at[q], s2dst.at[slot], s2ss.at[d], s2rs.at[slot], {"fsdp": dev}).start()

        each(1, NP, send)
        s2dst[slot] = s2src[p]

    advance(1, 3)

    each(1, NT, lambda d: copy(
        usend.at[:, 0], urecv.at[0], us.at[d], ur.at[d], {"tp": peer_t(d)}).wait_recv())
    summed = jnp.sum(urecv[...].astype(F32), axis=0).reshape(64, 256)
    u = summed[:, 0:128]
    lane = iota((64, 128), 1)
    sq = jnp.sum(
        jnp.where((lane == 0) | (lane == 64), summed[:, 128:256], 0.0), axis=1, keepdims=True
    )
    inv = lax.rsqrt(sq / D + 1e-06)
    zvals = inv * u + b_ref[...]
    kinv = lax.rsqrt(jnp.sum(zvals * zvals, axis=1, keepdims=True) + 1e-06)
    emb = zvals * kinv

    for i in range(4):
        @pl.when(jnp.logical_not(carries & (slot == i)))
        def _(i=i):
            copy(s2src.at[0], s2dst.at[i], s2ss.at[0], s2rs.at[i], {"fsdp": peer_p(1)[1]}).wait_recv()

    grads = permute_rows(
        64,
        lambda r: ((r >> 5) * 2 + ((r >> 1) & 1)) * 16 + ((r >> 2) & 7) * 2 + (r & 1),
        s2dst[...].reshape(64, 128),
    )
    row = iota((64, 128), 0)
    position = core * 256 + (row >> 5) * 128 + t * 32 + (row & 31)
    grads = jnp.where(position < len_ref[f // 2], grads, 0.0)
    dz = kinv * (grads - emb * jnp.sum(emb * grads, axis=1, keepdims=True))
    cvals = jnp.sum(dz * u, axis=1, keepdims=True)
    coef = inv * inv * inv * cvals / D
    inv_hi, inv_lo = split_hi_lo(inv)
    coef_hi, coef_lo = split_hi_lo(coef)
    tail = jnp.where(
        lane < 64,
        jnp.where(lane < 32, inv_hi, inv_lo),
        jnp.where(lane < 96, coef_hi, coef_lo),
    )
    dzp = dz.astype(BF)
    tailp = tail.astype(BF)
    for i in range(2):
        dzfull[i, t, :, 0:128] = dzp[i * 32 : i * 32 + 32]
        dzfull[i, t, :, 128:256] = tailp[i * 32 : i * 32 + 32]

    def send_dz(d):
        part = dzfull.at[:, t]
        copy(part, part, ds.at[d], dr.at[d], {"tp": peer_t(d)}).start()

    each(1, NT, send_dz)
    advance(3, 6)

    each(1, NT, lambda d: copy(
        dzfull.at[:, 0], dzfull.at[:, 0], ds.at[d], dr.at[d], {"tp": peer_t(d)}).wait_recv())
    dzall = dzfull[:, :, :, 0:128].reshape(256, 128).astype(F32)
    tails = dzfull[:, :, :, 128:256].reshape(256, 128).astype(F32)
    lane = iota((256, 128), 1)
    inv = jnp.sum(jnp.where((lane == 0) | (lane == 32), tails, 0.0), axis=1, keepdims=True)
    coef = jnp.sum(jnp.where((lane == 64) | (lane == 96), tails, 0.0), axis=1, keepdims=True)
    gain = g_ref[...]
    xv = x_ref[...].astype(F32)
    dn = jnp.dot(dzall, p_ref[...], precision=HIGH)
    dh = (inv * gain * dn - xv * coef).astype(BF)
    dhfull[t] = dh.reshape(2, 128, 512)
    tdev = ({"tp": (t + 1) % NT}, {"tp": (t + NT - 1) % NT})

    def dh_move(direction, h):
        part = dhfull.at[t, h]
        return copy(part, part, dhs.at[direction, h], dhr.at[direction, h], tdev[direction])

    for direction, h in ((0, 0), (1, 1), (0, 1), (1, 0)):
        dh_move(direction, h).start()

    xinv = xv * inv
    proj = lax.dot_general(dzall.T, xinv * gain, (((1,), (0,)), ((), ())), precision=HIGH) * (1.0 / 64.0)
    gsum = jnp.sum(dn * xinv, axis=0, keepdims=True) * (1.0 / 64.0)
    bsum = jnp.sum(dzall, axis=0, keepdims=True) * (1.0 / 64.0)
    row8 = iota((8, 128), 0)
    extra = jnp.where(row8 == 4, bsum, 0.0)
    for i in range(4):
        extra = jnp.where(row8 == i, gsum[:, i * 128 : i * 128 + 128], extra)

    def pack_extra(value):
        hi, lo = split_hi_lo(value)
        return jnp.concatenate([hi, lo], axis=0).astype(BF)

    main = jnp.concatenate(
        [proj[:, 0:256].reshape(16, 8, 256), proj[:, 256:512].reshape(16, 8, 256)], axis=1
    )
    rs_src[:, :, 0:256] = main.astype(BF)
    rs_src[:, :, 256:384] = jnp.broadcast_to(pack_extra(extra)[None], (16, 16, 128))

    def send_rs(d):
        q, dev = peer_p(d)
        copy(rs_src.at[q], rs_dst.at[p], rss.at[d], rsr.at[d], {"fsdp": dev}).start()

    each(1, NP, send_rs)
    rs_dst[p] = rs_src[p]
    advance(2, 6)

    def dh_forward(direction):
        part = dhfull.at[(t + NT - 1) % NT if direction == 0 else (t + 1) % NT, direction]
        return copy(part, part, dfs.at[direction], dfr.at[direction], tdev[direction])

    for direction in (0, 1):
        dh_move(direction, direction).wait_recv()
        dh_forward(direction).start()
    advance(2, 4)

    each(1, NP, lambda d: copy(
        rs_src.at[0], rs_dst.at[0], rss.at[d], rsr.at[d], {"fsdp": peer_p(d)[1]}).wait_recv())
    part = jnp.sum(rs_dst[...].astype(F32), axis=0)
    zbuf[z, :, 0:256] = part[:, 0:256].astype(BF)
    zbuf[z, :, 256:384] = pack_extra(part[0:8, 256:384] + part[8:16, 256:384])

    def send_z(d):
        q, dev = peer_z(d)
        copy(zbuf.at[z], zbuf.at[z], zss.at[d], zsr.at[d], {"fsdp": dev}).start()

    each(1, NZ, send_z)
    advance(2, 5)
    each(1, NZ, lambda d: copy(
        zbuf.at[0], zbuf.at[0], zss.at[d], zsr.at[d], {"fsdp": peer_z(d)[1]}).wait_recv())
    part = jnp.sum(zbuf[...].astype(F32), axis=0)
    ag[p] = part[:, 0:256].astype(BF)
    sums = part[0:8, 256:384] + part[8:16, 256:384]
    gain_ref[...] = sums[0:4]
    bias_ref[...] = sums[4:5]

    def send_ag(d):
        q, dev = peer_p(d)
        copy(ag.at[p], ag.at[p], ags.at[d], agr.at[d], {"fsdp": dev}).start()

    each(1, NP, send_ag)
    advance(len(todo0), len(todo1))

    for direction in (0, 1):
        dh_move(direction, 1 - direction).wait_recv()
        dh_forward(direction).wait_recv()
    copy(wfull.at[:, :, :, core], wfull.at[:, :, :, 1 - core], sibs, sibr, {"fsdp": f + 1 - 2 * core}).wait()
    dhv = jnp.concatenate([dhfull[i].reshape(256, 512) for i in range(4)], axis=1)
    for lo, hi in ((0, 512), (512, 1024), (1024, 1408)):
        act_ref[:, lo:hi] = jnp.dot(
            dhv, wfull[:, :, :, :, :, lo:hi].reshape(D, hi - lo), preferred_element_type=F32
        ).astype(BF)

    each(1, NP, lambda d: copy(
        ag.at[0], ag.at[0], ags.at[d], agr.at[d], {"fsdp": peer_p(d)[1]}).wait_recv())
    full = ag[...].astype(F32)
    proj_ref[:, 0:256] = full[:, 0:8].reshape(128, 256)
    proj_ref[:, 256:512] = full[:, 8:16].reshape(128, 256)

    def left_p(d):
        dev = {"fsdp": peer_p(d)[1]}
        copy(rs_src.at[0], rs_dst.at[0], rss.at[d], rsr.at[d], dev).wait_send()
        copy(ag.at[0], ag.at[0], ags.at[d], agr.at[d], dev).wait_send()

    def left_z(d):
        copy(zbuf.at[0], zbuf.at[0], zss.at[d], zsr.at[d], {"fsdp": peer_z(d)[1]}).wait_send()

    def left_t(d):
        dev = {"tp": peer_t(d)}
        copy(usend.at[:, 0], urecv.at[0], us.at[d], ur.at[d], dev).wait_send()
        copy(dzfull.at[:, 0], dzfull.at[:, 0], ds.at[d], dr.at[d], dev).wait_send()

    each(1, NP, left_p)
    each(1, NZ, left_z)
    each(1, NT, left_t)

    @pl.when(carries)
    def _():
        each(1, NZ, lambda d: copy(
            s1src.at[0], s1dst.at[0], s1ss.at[d], s1rs.at[d], {"fsdp": peer_z(d)[1]}).wait_send())
        each(1, NP, lambda d: copy(
            s2src.at[0], s2dst.at[0], s2ss.at[d], s2rs.at[0], {"fsdp": peer_p(d)[1]}).wait_send())

    for direction in (0, 1):
        dh_move(direction, 0).wait_send()
        dh_move(direction, 1).wait_send()
        dh_forward(direction).wait_send()

    @pl.when(core == 0)
    def _():
        for make in sends0:
            make().wait_send()

    @pl.when(core == 1)
    def _():
        for make in sends1:
            make().wait_send()


def shards(token_grads, hidden, proj_weight, proj_bias, norm_gain, down_weight, lengths):
    sem = pltpu.SemaphoreType.DMA
    vmem = pl.BlockSpec(memory_space=pltpu.VMEM)
    act, proj, gain, bias = pl.pallas_call(
        kernel,
        out_shape=(
            jax.ShapeDtypeStruct((256, 1408), BF),
            jax.ShapeDtypeStruct((128, 512), F32),
            jax.ShapeDtypeStruct((4, 128), F32),
            jax.ShapeDtypeStruct((1, 128), F32),
        ),
        in_specs=[vmem] * 6 + [pl.BlockSpec(memory_space=pltpu.SMEM)],
        out_specs=(vmem,) * 4,
        scratch_shapes=[
            pltpu.VMEM((2, NX, NZ, 2, 16, 1408), BF),
            pltpu.VMEM((2, NT, 32, 256), BF),
            pltpu.VMEM((NT, 2, 32, 256), BF),
            pltpu.VMEM((NZ, 32, 128), BF),
            pltpu.VMEM((NZ, 32, 128), BF),
            pltpu.VMEM((NP, 16, 128), BF),
            pltpu.VMEM((4, 16, 128), BF),
            pltpu.VMEM((2, NT, 32, 256), BF),
            pltpu.VMEM((NT, 2, 128, 512), BF),
            pltpu.VMEM((NP, 16, 384), BF),
            pltpu.VMEM((NP, 16, 384), BF),
            pltpu.VMEM((NZ, 16, 384), BF),
            pltpu.VMEM((NP, 16, 256), BF),
            sem((NG,)), sem((NG,)),
            sem((2, 4, 2)), sem((2, 4, 2)),
            sem, sem,
            sem((2, 4)), sem((2, 4)),
            sem((2, 8)), sem((2, 8)),
            sem((8,)), sem((8,)),
            sem, sem,
            sem((NZ,)), sem((NZ,)),
            sem((NP,)), sem((4,)),
            sem((NT,)), sem((NT,)),
            sem((NT,)), sem((NT,)),
            sem((2, 2)), sem((2, 2)),
            sem((2,)), sem((2,)),
            sem((NP,)), sem((NP,)),
            sem((NZ,)), sem((NZ,)),
            sem((NP,)), sem((NP,)),
        ],
        compiler_params=pltpu.CompilerParams(
            collective_id=0, has_side_effects=True, vmem_limit_bytes=48 * 1024 * 1024
        ),
    )(
        token_grads, hidden, proj_weight, proj_bias.reshape(1, 128), norm_gain.reshape(1, 512),
        down_weight.T, lengths,
    )
    return act, proj, gain.reshape(512), bias.reshape(128)


def solution(mesh):
    placed = (P("fsdp", None), P("fsdp", "tp"), P(None, "tp"), P(), P("tp"), P("tp", "fsdp"), P())
    return jax.shard_map(
        shards,
        mesh=mesh,
        in_specs=placed,
        out_specs=(P("fsdp", "tp"), P(None, "tp"), P("tp"), P()),
        check_vma=False,
    )
```

```python
import jax
import jax.numpy as jnp
from jax import lax
from jax.experimental import pallas as pl
from jax.experimental.pallas import tpu as pltpu
from jax.sharding import PartitionSpec as P

D = 2048
LEN = 512
NX, NZ, NG, NP, NT = 4, 8, 8, 16, 4
HIDL, HIDP = 1408, 1536
YREC, XREC = 28, {1: 29, 2: 30, 3: 31, 5: 56, 6: 57, 7: 58}
VLIM = 56 * 1024 * 1024
MESH = pl.DeviceIdType.MESH
HIGH = lax.Precision.HIGHEST
BF, F32, I32 = jnp.bfloat16, jnp.float32, jnp.int32
NT_DIMS = (((1,), (1,)), ((), ()))


def iota(shape, axis):
    return lax.broadcasted_iota(I32, shape, axis)


def split_hi_lo(value):
    hi = value.astype(BF).astype(F32)
    return hi, value - hi


def permute_rows(count, source_of, rows):
    hot = jnp.where(
        iota((count, count), 1) == source_of(iota((count, count), 0)), F32(1.0), F32(0.0)
    ).astype(BF)
    return jnp.dot(hot, rows, preferred_element_type=F32)


def kernel(
    tg_hbm, x_hbm, p_hbm, b_hbm, g_hbm, w_hbm, len_hbm,
    act_out, proj_out, gain_out, bias_out,
    act_ref, proj_ref, gain_ref, bias_ref, outs,
    tg_ref, xfull, p_ref, b_ref, g_ref, w_ref, len_ref,
    wfull, pgt, usend, urecv, s1src, s1dst, s2src, s2dst, dzfull, dhv, rs_src, rs_dst, zbuf, ag,
    ins, ringsend, sidesend, wr, sibs, sibr,
    s1ss, s1rs, s2ss, s2rs, us, ur, ps, pr, ds, dr, dhs, dhr, dfr, rss, rsr, zss, zsr, ags, agr,
):
    f = lax.axis_index("fsdp")
    t = lax.axis_index("tp")
    core = f % 2
    z = (f // 2) % NZ
    grp = f // 16
    xa = grp % NX
    yl = grp // NX
    p = f % 16

    def at_f(group, zpos, cpos):
        return group * 16 + zpos * 2 + cpos

    def peer_p(d):
        q = (p + d) % NP
        return q, grp * 16 + q

    def peer_g(d):
        q = (grp + d) % NG
        return q, q * 16 + p

    def peer_t(d):
        return (t + d) % NT

    def copy(src, dst, ssem, rsem, dev):
        return pltpu.make_async_remote_copy(
            src_ref=src, dst_ref=dst, send_sem=ssem, recv_sem=rsem,
            device_id=dev, device_id_type=MESH,
        )

    def each(lo, hi, body):
        def step(d, carry):
            body(d)
            return carry

        lax.fori_loop(lo, hi, step, 0)

    loads = [
        pltpu.make_async_copy(src, dst, ins.at[i])
        for i, (src, dst) in enumerate((
            (w_hbm, w_ref), (tg_hbm, tg_ref), (x_hbm, xfull.at[t]), (p_hbm, p_ref),
            (g_hbm, g_ref), (b_hbm, b_ref), (len_hbm, len_ref),
        ))
    ]
    for load in loads:
        load.start()

    near_p = {"fsdp": peer_p(1)[1]}
    near_g = {"fsdp": peer_g(1)[1]}

    bar = pltpu.get_barrier_semaphore()

    def greet(dev):
        pl.semaphore_signal(bar, inc=1, device_id=dev, device_id_type=MESH)

    each(1, NP, lambda d: greet({"fsdp": peer_p(d)[1]}))
    each(1, NG, lambda d: greet({"fsdp": peer_g(d)[1]}))
    each(1, NT, lambda d: greet({"tp": peer_t(d)}))

    loads[0].wait()
    wfull[yl, xa, z, core, :, 0:HIDL] = w_ref[...].astype(BF)
    loads[1].wait()
    carries = grp // 2 == t

    @pl.when(carries)
    def _():
        rows = permute_rows(
            256, lambda r: ((r >> 1) & 7) * 32 + (r >> 4) * 2 + (r & 1), tg_ref[...].astype(BF)
        )
        s1src[...] = rows.astype(BF).reshape(16, 16, 128)

    for load in loads[2:]:
        load.wait()
    gain = g_ref[...]
    pg = p_ref[...] * gain
    pg_hi = pg.astype(BF)
    pg_lo = (pg - pg_hi.astype(F32)).astype(BF)
    pgt[...] = pg.T.astype(BF).reshape(32, 16, 128)
    pl.semaphore_wait(bar, (NP - 1) + (NG - 1) + (NT - 1))

    def go(make):
        make().start()

    def sibling(piece):
        copy(piece, piece, sibs, sibr, {"fsdp": f + 1 - 2 * core}).start()

    own = wfull.at[yl, xa, z, core]
    met = wfull.at[1 - yl, xa, z, core]
    own_p = wfull.at[yl, xa, z, core, :, pl.ds(HIDL, 128)]
    zdev = ({"fsdp": at_f(grp, (z + 1) % NZ, core)}, {"fsdp": at_f(grp, (z + NZ - 1) % NZ, core)})
    xdev = (
        {"fsdp": at_f(yl * NX + (xa + 1) % NX, z, core)},
        {"fsdp": at_f(yl * NX + (xa + NX - 1) % NX, z, core)},
    )

    ydev = {"fsdp": at_f((grp + NX) % NG, z, core)}

    def zslot(direction, s):
        return (z + NZ - s) % NZ if direction == 0 else (z + s) % NZ

    def piece0(i, zj):
        return wfull.at[yl if i < NX else 1 - yl, (xa + i % NX) % NX, zj, 0]

    def xdev_at(d):
        return {"fsdp": at_f(yl * NX + (xa + d) % NX, z, core)}

    def zmove0(direction, s, i):
        def make():
            piece = piece0(i, zslot(direction, s))
            return copy(piece, piece, ringsend, wr.at[direction * 32 + s * 8 + i], zdev[direction])

        return make

    def launch0(i):
        for direction in (0, 1):
            go(zmove0(direction, 0, i))
        sibling(piece0(i, z))

    def begin0():
        go(lambda: copy(own, own, sidesend, wr.at[YREC], ydev))
        for d in range(1, NX):
            go(lambda d=d: copy(own, own, sidesend, wr.at[XREC[d]], xdev_at(NX - d)))
        launch0(0)

    def relay0():
        copy(met, met, sidesend, wr.at[YREC], ydev).wait_recv()
        for d in range(1, NX):
            go(lambda d=d: copy(met, met, sidesend, wr.at[XREC[NX + d]], xdev_at(NX - d)))
        launch0(NX)

    def ring0(i):
        def run():
            copy(own, own, sidesend, wr.at[XREC[i]], zdev[0]).wait_recv()
            launch0(i)

        return run

    def arrive0(s, direction, i):
        zmove0(direction, s - 1, i)().wait_recv()
        if s < 3 or (s == 3 and (i < NX) == (direction == 0)):
            go(zmove0(direction, s, i))
        sibling(piece0(i, zslot(direction, s)))

    def step0(s, i):
        def run():
            if s < 4 or i < NX:
                arrive0(s, 0, i)
            if s < 4:
                arrive0(s, 1, i)
            elif i < NX:
                arrive0(s, 1, i + NX)

        return run

    todo0 = [begin0, ring0(1), ring0(3), ring0(2), relay0, step0(1, 0), ring0(5), ring0(7), ring0(6)]
    order = (1, 3, 2, 4, 5, 7, 6)
    todo0 += [step0(1, i) for i in order]
    todo0 += [step0(2, i) for i in (0,) + order] + [step0(3, i) for i in (0,) + order]
    todo0 += [step0(4, i) for i in (0, 1, 3, 2)]

    hops = [(0, 0), (0, 1), (1, 1), (0, 2), (1, 2), (0, 3), (1, 3), (0, 4)]

    def piece1(xj, zj):
        return wfull.at[:, xj, zj, 1]

    def zmove1(direction, s):
        def make():
            piece = piece1(xa, zslot(direction, s))
            return copy(piece, piece, ringsend, wr.at[direction * 4 + s], zdev[direction])

        return make

    def xmove(direction, k):
        def make():
            piece = piece1(xa, zslot(*hops[k]))
            return copy(piece, piece, sidesend, wr.at[8 + direction * 8 + k], xdev[direction])

        return make

    def xforward(k):
        direction = k % 2

        def make():
            xj = (xa + NX - 1) % NX if direction == 0 else (xa + 1) % NX
            piece = piece1(xj, zslot(*hops[k]))
            return copy(piece, piece, sidesend, wr.at[24 + k], xdev[direction])

        return make

    def begin1():
        go(lambda: copy(own, own, ringsend, wr.at[32], ydev))

    def spread(k):
        go(xmove(0, k))
        go(xmove(1, k))
        sibling(piece1(xa, zslot(*hops[k])))

    def first1():
        copy(met, met, ringsend, wr.at[32], ydev).wait_recv()
        go(zmove1(0, 0))
        go(zmove1(1, 0))
        spread(0)

    def zstep1(k):
        def run():
            direction, s = hops[k]
            zmove1(direction, s - 1)().wait_recv()
            if s < 3 or (s == 3 and direction == 0):
                go(zmove1(direction, s))
            spread(k)

        return run

    def xstep1(k, direction):
        def run():
            xmove(direction, k)().wait_recv()
            xj = (xa + NX - 1) % NX if direction == 0 else (xa + 1) % NX
            if k % 2 == direction:
                go(xforward(k))
            sibling(piece1(xj, zslot(*hops[k])))

        return run

    def fstep1(k):
        def run():
            xforward(k)().wait_recv()
            sibling(piece1((xa + 2) % NX, zslot(*hops[k])))

        return run

    todo1 = [begin1, first1]
    for k in range(1, 8):
        todo1.append(zstep1(k))
        if k >= 3:
            todo1 += [xstep1(k - 3, 0), xstep1(k - 3, 1)]
        if k >= 6:
            todo1.append(fstep1(k - 6))
    for k in (5, 6, 7):
        todo1 += [xstep1(k, 0), xstep1(k, 1), fstep1(k - 3)]
    todo1 += [fstep1(k) for k in (5, 6, 7)]

    def advance(n0, n1):
        head0, head1 = todo0[:n0], todo1[:n1]
        del todo0[:n0], todo1[:n1]
        if head0:
            @pl.when(core == 0)
            def _():
                for run in head0:
                    run()
        if head1:
            @pl.when(core == 1)
            def _():
                for run in head1:
                    run()

    p_slab = f // 32
    p_row = f % 32
    p_src = pgt.at[p_row]

    @pl.when(p_slab == t)
    def _():
        def send(d):
            copy(p_src, own_p, ps, pr, {"tp": peer_t(d)}).start()

        each(1, NT, send)
        wfull[yl, xa, z, core, :, HIDL:HIDP] = pgt[p_row]

    @pl.when(carries)
    def _():
        def send(d):
            q, dev = peer_p(d)
            copy(s1src.at[q], s1dst.at[p], s1ss, s1rs, {"fsdp": dev}).start()

        each(1, NP, send)
        s1dst[p] = s1src[p]

    xv = xfull[t].reshape(256, 512)
    pu = lax.dot_general(xv, pg_hi, NT_DIMS, preferred_element_type=F32)
    pu = pu + lax.dot_general(xv, pg_lo, NT_DIMS, preferred_element_type=F32)
    xv = xv.astype(F32)
    sq_hi, sq_lo = split_hi_lo(jnp.sum(xv * xv, axis=1, keepdims=True))
    sq2 = jnp.where(iota((256, 128), 1) < 64, sq_hi, sq_lo)
    usend[:, :, 0:128] = pu.astype(BF).reshape(4, 64, 128)
    usend[:, :, 128:256] = sq2.astype(BF).reshape(4, 64, 128)

    def send_u(d):
        q = peer_t(d)
        copy(usend.at[q], urecv.at[t], us, ur, {"tp": q}).start()

    each(1, NT, send_u)
    urecv[t] = usend[t]

    tdev = ({"tp": (t + 1) % NT}, {"tp": (t + NT - 1) % NT})

    def x_move(direction, h):
        part = xfull.at[t, h]
        return copy(part, part, dhs, dhr.at[direction, h], tdev[direction])

    def x_forward(direction):
        part = xfull.at[(t + NT - 1) % NT if direction == 0 else (t + 1) % NT, direction]
        return copy(part, part, dhs, dfr.at[direction], tdev[direction])

    @pl.when(p_slab != t)
    def _():
        copy(p_src, own_p, ps, pr, tdev[0]).wait_recv()

    advance(1, 1)

    slot = grp % 2

    @pl.when(carries)
    def _():
        copy(s1src.at[0:15], s1dst.at[0:15], s1ss, s1rs, near_p).wait_recv()
        rows = permute_rows(
            256,
            lambda r: ((r >> 1) & 15) * 16 + (r >> 5) * 2 + (r & 1),
            s1dst[...].reshape(256, 128),
        )
        s2src[...] = rows.astype(BF).reshape(8, 32, 128)

        def send(d):
            q, dev = peer_g(d)
            copy(s2src.at[q], s2dst.at[slot], s2ss, s2rs.at[slot], {"fsdp": dev}).start()

        each(1, NG, send)
        s2dst[slot] = s2src[grp]

    advance(3, 1)

    copy(usend.at[0:3], urecv.at[0:3], us, ur, tdev[0]).wait_recv()
    summed = jnp.sum(urecv[...].astype(F32), axis=0)
    u = summed[:, 0:128]
    lane = iota((64, 128), 1)
    sq = jnp.sum(
        jnp.where((lane == 0) | (lane == 64), summed[:, 128:256], 0.0), axis=1, keepdims=True
    )
    inv = lax.rsqrt(sq / D + 1e-06)
    zvals = inv * u + b_ref[...]
    kinv = lax.rsqrt(jnp.sum(zvals * zvals, axis=1, keepdims=True) + 1e-06)
    emb = zvals * kinv
    advance(0, 1)

    for i in range(2):
        @pl.when(jnp.logical_not(carries & (slot == i)))
        def _(i=i):
            copy(s2src.at[0], s2dst.at[i], s2ss, s2rs.at[i], {"fsdp": peer_g(1)[1]}).wait_recv()

    position = core * 256 + t * 64 + iota((64, 128), 0)
    grads = jnp.where(
        position < len_ref[f // 2], s2dst[...].reshape(64, 128).astype(F32), 0.0
    )
    dz = kinv * (grads - emb * jnp.sum(emb * grads, axis=1, keepdims=True))
    cvals = jnp.sum(dz * u, axis=1, keepdims=True)
    coef = inv * inv * inv * cvals / D
    inv_hi, inv_lo = split_hi_lo(inv)
    coef_hi, coef_lo = split_hi_lo(coef)
    tail = jnp.where(
        lane < 64,
        jnp.where(lane < 32, inv_hi, inv_lo),
        jnp.where(lane < 96, coef_hi, coef_lo),
    )
    dzfull[t, :, 0:128] = dz.astype(BF)
    dzfull[t, :, 128:256] = tail.astype(BF)

    def send_dz(d):
        part = dzfull.at[t]
        copy(part, part, ds, dr, {"tp": peer_t(d)}).start()

    each(1, NT, send_dz)
    advance(12, 2)

    copy(dzfull.at[0:3], dzfull.at[0:3], ds, dr, tdev[0]).wait_recv()
    dzall = dzfull[:, :, 0:128].reshape(256, 128)
    tails = dzfull[:, :, 128:256].reshape(256, 128).astype(F32)
    lane = iota((256, 128), 1)
    inv = jnp.sum(jnp.where((lane == 0) | (lane == 32), tails, 0.0), axis=1, keepdims=True)
    coef = jnp.sum(jnp.where((lane == 64) | (lane == 96), tails, 0.0), axis=1, keepdims=True)
    dzf = dzall.astype(F32)
    xinv = (xfull[t].reshape(256, 512).astype(F32) * (inv * (1.0 / 64.0))).astype(BF)
    sums = jnp.dot(dzf.T.astype(BF), xinv, preferred_element_type=F32)
    bsum = jnp.sum(dzf, axis=0, keepdims=True) * (1.0 / 64.0)
    row8 = iota((8, 128), 0)
    extra = jnp.where(row8 == 0, bsum, 0.0)

    def pack_extra(value):
        hi, lo = split_hi_lo(value)
        return jnp.concatenate([hi, lo], axis=0).astype(BF)

    main = jnp.concatenate(
        [sums[:, 0:256].reshape(16, 8, 256), sums[:, 256:512].reshape(16, 8, 256)], axis=1
    )
    rs_src[:, :, 0:256] = main.astype(BF)
    rs_src[:, :, 256:384] = jnp.broadcast_to(pack_extra(extra)[None], (16, 16, 128))

    def send_rs(d):
        q, dev = peer_p(d)
        copy(rs_src.at[q], rs_dst.at[p], rss, rsr, {"fsdp": dev}).start()

    each(1, NP, send_rs)
    rs_dst[p] = rs_src[p]
    for direction, h in ((0, 0), (1, 1), (0, 1), (1, 0)):
        x_move(direction, h).start()
    advance(8, 9)
    for direction in (0, 1):
        x_move(direction, direction).wait_recv()
        x_forward(direction).start()
    advance(4, 11)

    copy(rs_src.at[0:15], rs_dst.at[0:15], rss, rsr, near_p).wait_recv()
    part = jnp.sum(rs_dst[...].astype(F32), axis=0)
    zbuf[grp, :, 0:256] = part[:, 0:256].astype(BF)
    zbuf[grp, :, 256:384] = pack_extra(part[0:8, 256:384] + part[8:16, 256:384])

    def send_z(d):
        q, dev = peer_g(d)
        copy(zbuf.at[grp], zbuf.at[grp], zss, zsr, {"fsdp": dev}).start()

    each(1, NG, send_z)
    advance(4, 4)
    copy(zbuf.at[0:7], zbuf.at[0:7], zss, zsr, near_g).wait_recv()
    part = jnp.sum(zbuf[...].astype(F32), axis=0)
    ag[p] = part[:, 0:256].astype(BF)
    bias_ref[...] = (part[0:8, 256:384] + part[8:16, 256:384])[0:1]

    def send_ag(d):
        q, dev = peer_p(d)
        copy(ag.at[p], ag.at[p], ags, agr, {"fsdp": dev}).start()

    each(1, NP, send_ag)
    advance(len(todo0), len(todo1))

    for direction in (0, 1):
        x_move(direction, 1 - direction).wait_recv()
        x_forward(direction).wait_recv()
    copy(wfull.at[:, :, :, core], wfull.at[:, :, :, 1 - core], sibs, sibr, {"fsdp": f + 1 - 2 * core}).wait()
    for j in range(NT):
        for k in range(2):
            pgt_part = wfull[j // 2, (j % 2) * 2 + k, :, :, :, HIDL:HIDP].reshape(256, 128)
            dn = lax.dot_general(dzall, pgt_part, NT_DIMS, preferred_element_type=F32)
            xpart = xfull[j, :, :, k * 256 : k * 256 + 256].reshape(256, 256).astype(F32)
            lo = j * 512 + k * 256
            dhv[:, lo : lo + 256] = (inv * dn - xpart * coef).astype(BF)
    stores = []

    def store(src, dst):
        move = pltpu.make_async_copy(src, dst, outs.at[len(stores)])
        move.start()
        stores.append(move)

    store(bias_ref, bias_out)
    for lo, hi in ((0, 512), (512, 1024), (1024, 1408)):
        act_ref[:, lo:hi] = jnp.dot(
            dhv[...], wfull[:, :, :, :, :, lo:hi].reshape(D, hi - lo), preferred_element_type=F32
        ).astype(BF)
        store(act_ref.at[:, lo:hi], act_out.at[:, lo:hi])

    copy(rs_src.at[0:15], rs_dst.at[0:15], rss, rsr, near_p).wait_send()
    copy(zbuf.at[0:7], zbuf.at[0:7], zss, zsr, near_g).wait_send()
    copy(usend.at[0:3], urecv.at[0:3], us, ur, tdev[0]).wait_send()
    copy(dzfull.at[0:3], dzfull.at[0:3], ds, dr, tdev[0]).wait_send()
    copy(xfull.at[0:3], xfull.at[0:3], dhs, dfr.at[0], tdev[0]).wait_send()

    @pl.when(p_slab == t)
    def _():
        copy(pgt.at[0:3], pgt.at[0:3], ps, pr, tdev[0]).wait_send()

    @pl.when(carries)
    def _():
        copy(s1src.at[0:15], s1dst.at[0:15], s1ss, s1rs, near_p).wait_send()
        copy(s2src.at[0:7], s2src.at[0:7], s2ss, s2rs.at[0], near_g).wait_send()

    def all_left(part, send_sem):
        copy(part, part, send_sem, wr.at[0], zdev[0]).wait_send()

    @pl.when(core == 0)
    def _():
        all_left(wfull.at[:, :, 0:7, 0], ringsend)
        all_left(wfull.at[0, 0, 0:7, 0], sidesend)

    @pl.when(core == 1)
    def _():
        all_left(wfull.at[0, 0:3, 0:5, 1], ringsend)
        all_left(wfull.at[:, 0:3, :, 1], sidesend)

    copy(ag.at[0:15], ag.at[0:15], ags, agr, near_p).wait()
    full = ag[...].astype(F32)
    full = jnp.concatenate(
        [full[:, 0:8].reshape(128, 256), full[:, 8:16].reshape(128, 256)], axis=1
    )
    proj_ref[...] = full * gain
    gain_ref[...] = jnp.sum(full * p_ref[...], axis=0, keepdims=True)
    store(proj_ref, proj_out)
    store(gain_ref, gain_out)

    for move in stores:
        move.wait()


def shards(token_grads, hidden, proj_weight, proj_bias, norm_gain, down_weight, lengths):
    sem = pltpu.SemaphoreType.DMA
    anywhere = pl.BlockSpec(memory_space=pl.ANY)
    results = (
        jax.ShapeDtypeStruct((256, HIDL), BF),
        jax.ShapeDtypeStruct((128, 512), F32),
        jax.ShapeDtypeStruct((1, 512), F32),
        jax.ShapeDtypeStruct((1, 128), F32),
    )
    act, proj, gain, bias = pl.pallas_call(
        kernel,
        out_shape=results,
        in_specs=[anywhere] * 7,
        out_specs=(anywhere,) * 4,
        scratch_shapes=[
            pltpu.VMEM((256, HIDL), BF),
            pltpu.VMEM((128, 512), F32),
            pltpu.VMEM((1, 512), F32),
            pltpu.VMEM((1, 128), F32),
            sem((6,)),
            pltpu.VMEM((256, 128), F32),
            pltpu.VMEM((NT, 2, 128, 512), BF),
            pltpu.VMEM((128, 512), F32),
            pltpu.VMEM((1, 128), F32),
            pltpu.VMEM((1, 512), F32),
            pltpu.VMEM((16, HIDL), F32),
            pltpu.SMEM((64,), I32),
            pltpu.VMEM((2, NX, NZ, 2, 16, HIDP), BF),
            pltpu.VMEM((32, 16, 128), BF),
            pltpu.VMEM((NT, 64, 256), BF),
            pltpu.VMEM((NT, 64, 256), BF),
            pltpu.VMEM((NP, 16, 128), BF),
            pltpu.VMEM((NP, 16, 128), BF),
            pltpu.VMEM((NG, 32, 128), BF),
            pltpu.VMEM((2, 32, 128), BF),
            pltpu.VMEM((NT, 64, 256), BF),
            pltpu.VMEM((256, D), BF),
            pltpu.VMEM((NP, 16, 384), BF),
            pltpu.VMEM((NP, 16, 384), BF),
            pltpu.VMEM((NG, 16, 384), BF),
            pltpu.VMEM((NP, 16, 256), BF),
            sem((7,)),
            sem, sem, sem((64,)), sem, sem,
            sem, sem, sem, sem((2,)),
            sem, sem, sem, sem,
            sem, sem,
            sem, sem((2, 2)), sem((2,)),
            sem, sem, sem, sem, sem, sem,
        ],
        compiler_params=pltpu.CompilerParams(
            collective_id=0, has_side_effects=True, vmem_limit_bytes=VLIM
        ),
    )(
        token_grads, hidden.reshape(2, 128, 512), proj_weight, proj_bias.reshape(1, 128),
        norm_gain.reshape(1, 512), down_weight.T, lengths,
    )
    return act, proj, gain.reshape(512), bias.reshape(128)


def solution(mesh):
    placed = (P("fsdp", None), P("fsdp", "tp"), P(None, "tp"), P(), P("tp"), P("tp", "fsdp"), P())
    return jax.shard_map(
        shards,
        mesh=mesh,
        in_specs=placed,
        out_specs=(P("fsdp", "tp"), P(None, "tp"), P("tp"), P()),
        check_vma=False,
    )
```

```python
import jax
import jax.numpy as jnp
from jax import lax
from jax.experimental import pallas as pl
from jax.experimental.pallas import tpu as pltpu
from jax.sharding import PartitionSpec as P

D = 2048
LEN = 512
NX, NZ, NG, NP, NT = 4, 8, 8, 16, 4
HIDL, HIDP = 1408, 1536
YREC, XREC = 28, {1: 29, 2: 30, 3: 31, 5: 56, 6: 57, 7: 58}
VLIM = 56 * 1024 * 1024
MESH = pl.DeviceIdType.MESH
HIGH = lax.Precision.HIGHEST
BF, F32, I32 = jnp.bfloat16, jnp.float32, jnp.int32
NT_DIMS = (((1,), (1,)), ((), ()))


def iota(shape, axis):
    return lax.broadcasted_iota(I32, shape, axis)


def split_hi_lo(value):
    hi = value.astype(BF).astype(F32)
    return hi, value - hi


def permute_rows(count, source_of, rows):
    hot = jnp.where(
        iota((count, count), 1) == source_of(iota((count, count), 0)), F32(1.0), F32(0.0)
    ).astype(BF)
    return jnp.dot(hot, rows, preferred_element_type=F32)


def kernel(
    tg_hbm, x_hbm, p_hbm, b_hbm, g_hbm, w_hbm, len_hbm,
    act_out, proj_out, gain_out, bias_out,
    act_ref, proj_ref, gain_ref, bias_ref, outs,
    tg_ref, xfull, p_ref, b_ref, g_ref, w_ref, len_ref,
    wfull, pgt, usend, urecv, s1src, s1dst, s2src, s2dst, dzfull, dhv, rs_src, rs_dst, zbuf, ag,
    ins, ringsend, sidesend, wr, sibs, sibr,
    s1ss, s1rs, s2ss, s2rs, us, ur, ps, pr, ds, dr, dhs, dhr, dfr, rss, rsr, zss, zsr, ags, agr,
):
    f = lax.axis_index("fsdp")
    t = lax.axis_index("tp")
    core = f % 2
    z = (f // 2) % NZ
    grp = f // 16
    xa = grp % NX
    yl = grp // NX
    p = f % 16

    def at_f(group, zpos, cpos):
        return group * 16 + zpos * 2 + cpos

    def peer_p(d):
        q = (p + d) % NP
        return q, grp * 16 + q

    def peer_g(d):
        q = (grp + d) % NG
        return q, q * 16 + p

    def peer_t(d):
        return (t + d) % NT

    def copy(src, dst, ssem, rsem, dev):
        return pltpu.make_async_remote_copy(
            src_ref=src, dst_ref=dst, send_sem=ssem, recv_sem=rsem,
            device_id=dev, device_id_type=MESH,
        )

    def each(lo, hi, body):
        def step(d, carry):
            body(d)
            return carry

        lax.fori_loop(lo, hi, step, 0)

    loads = [
        pltpu.make_async_copy(src, dst, ins.at[i])
        for i, (src, dst) in enumerate((
            (w_hbm, w_ref), (tg_hbm, tg_ref), (x_hbm, xfull.at[t]), (p_hbm, p_ref),
            (g_hbm, g_ref), (b_hbm, b_ref), (len_hbm, len_ref),
        ))
    ]
    for load in loads:
        load.start()

    near_p = {"fsdp": peer_p(1)[1]}
    near_g = {"fsdp": peer_g(1)[1]}

    bar = pltpu.get_barrier_semaphore()

    def greet(dev):
        pl.semaphore_signal(bar, inc=1, device_id=dev, device_id_type=MESH)

    each(1, NP, lambda d: greet({"fsdp": peer_p(d)[1]}))
    each(1, NG, lambda d: greet({"fsdp": peer_g(d)[1]}))
    each(1, NT, lambda d: greet({"tp": peer_t(d)}))

    loads[0].wait()
    wfull[yl, xa, z, core, :, 0:HIDL] = w_ref[...].astype(BF)
    loads[1].wait()
    carries = grp // 2 == t

    @pl.when(carries)
    def _():
        rows = permute_rows(
            256, lambda r: ((r >> 1) & 7) * 32 + (r >> 4) * 2 + (r & 1), tg_ref[...].astype(BF)
        )
        s1src[...] = rows.astype(BF).reshape(16, 16, 128)

    for load in loads[2:]:
        load.wait()
    gain = g_ref[...]
    pg = p_ref[...] * gain
    pg_hi = pg.astype(BF)
    pg_lo = (pg - pg_hi.astype(F32)).astype(BF)
    pgt[...] = pg.T.astype(BF).reshape(32, 16, 128)
    pl.semaphore_wait(bar, (NP - 1) + (NG - 1) + (NT - 1))

    def go(make):
        make().start()

    def sibling(piece):
        copy(piece, piece, sibs, sibr, {"fsdp": f + 1 - 2 * core}).start()

    own = wfull.at[yl, xa, z, core]
    met = wfull.at[1 - yl, xa, z, core]
    met_w = wfull.at[1 - yl, xa, z, core, :, pl.ds(0, HIDL)]
    met_p = wfull.at[1 - yl, xa, z, core, :, pl.ds(HIDL, 128)]
    own_w = wfull.at[yl, xa, z, core, :, pl.ds(0, HIDL)]
    own_p = wfull.at[yl, xa, z, core, :, pl.ds(HIDL, 128)]
    zdev = ({"fsdp": at_f(grp, (z + 1) % NZ, core)}, {"fsdp": at_f(grp, (z + NZ - 1) % NZ, core)})
    xdev = (
        {"fsdp": at_f(yl * NX + (xa + 1) % NX, z, core)},
        {"fsdp": at_f(yl * NX + (xa + NX - 1) % NX, z, core)},
    )

    ydev = {"fsdp": at_f((grp + NX) % NG, z, core)}

    def zslot(direction, s):
        return (z + NZ - s) % NZ if direction == 0 else (z + s) % NZ

    def piece0(i, zj):
        return wfull.at[yl if i < NX else 1 - yl, (xa + i % NX) % NX, zj, 0]

    def xdev_at(d):
        return {"fsdp": at_f(yl * NX + (xa + d) % NX, z, core)}

    def zmove0(direction, s, i):
        def make():
            piece = piece0(i, zslot(direction, s))
            return copy(piece, piece, ringsend, wr.at[direction * 32 + s * 8 + i], zdev[direction])

        return make

    def launch0(i):
        for direction in (0, 1):
            go(zmove0(direction, 0, i))
        sibling(piece0(i, z))

    def begin0(part, yrec):
        go(lambda: copy(part, part, sidesend, wr.at[yrec], ydev))
        for d in range(1, NX):
            go(lambda d=d: copy(part, part, sidesend, wr.at[XREC[d]], xdev_at(NX - d)))
        for direction in (0, 1):
            go(lambda: copy(part, part, ringsend, wr.at[direction * 32], zdev[direction]))

    def end_begin0():
        begin0(own_p, YREC + 31)
        sibling(own)

    def relay0(part, yrec):
        copy(part, part, sidesend, wr.at[yrec], ydev).wait_recv()
        for d in range(1, NX):
            go(lambda d=d: copy(part, part, sidesend, wr.at[XREC[NX + d]], xdev_at(NX - d)))
        for direction in (0, 1):
            go(lambda: copy(part, part, ringsend, wr.at[direction * 32 + NX], zdev[direction]))

    def end_relay0():
        relay0(met_p, YREC + 31)
        sibling(met)

    def ring0(i):
        def run():
            copy(own, own, sidesend, wr.at[XREC[i]], zdev[0]).wait_recv()
            launch0(i)

        return run

    def arrive0(s, direction, i):
        zmove0(direction, s - 1, i)().wait_recv()
        if s < 3 or (s == 3 and (i < NX) == (direction == 0)):
            go(zmove0(direction, s, i))
        sibling(piece0(i, zslot(direction, s)))

    def step0(s, i):
        def run():
            if s < 4 or i < NX:
                arrive0(s, 0, i)
            if s < 4:
                arrive0(s, 1, i)
            elif i < NX:
                arrive0(s, 1, i + NX)

        return run

    todo0 = [lambda: begin0(own_w, YREC), end_begin0, lambda: relay0(met_w, YREC)]
    todo0 += [ring0(1), ring0(3), ring0(2), end_relay0, step0(1, 0), ring0(5), ring0(7), ring0(6)]
    order = (1, 3, 2, 4, 5, 7, 6)
    todo0 += [step0(1, i) for i in order]
    todo0 += [step0(2, i) for i in (0,) + order] + [step0(3, i) for i in (0,) + order]
    todo0 += [step0(4, i) for i in (0, 1, 3, 2)]

    hops = [(0, 0), (0, 1), (1, 1), (0, 2), (1, 2), (0, 3), (1, 3), (0, 4)]

    def piece1(xj, zj):
        return wfull.at[:, xj, zj, 1]

    def zmove1(direction, s):
        def make():
            piece = piece1(xa, zslot(direction, s))
            return copy(piece, piece, ringsend, wr.at[direction * 4 + s], zdev[direction])

        return make

    def xmove(direction, k):
        def make():
            piece = piece1(xa, zslot(*hops[k]))
            return copy(piece, piece, sidesend, wr.at[8 + direction * 8 + k], xdev[direction])

        return make

    def xforward(k):
        direction = k % 2

        def make():
            xj = (xa + NX - 1) % NX if direction == 0 else (xa + 1) % NX
            piece = piece1(xj, zslot(*hops[k]))
            return copy(piece, piece, sidesend, wr.at[24 + k], xdev[direction])

        return make

    def begin1(part):
        go(lambda: copy(part, part, ringsend, wr.at[32], ydev))

    def spread(k):
        go(xmove(0, k))
        go(xmove(1, k))
        sibling(piece1(xa, zslot(*hops[k])))

    def first1():
        copy(met, met, ringsend, wr.at[32], ydev).wait_recv()
        go(zmove1(0, 0))
        go(zmove1(1, 0))
        spread(0)

    def zstep1(k):
        def run():
            direction, s = hops[k]
            zmove1(direction, s - 1)().wait_recv()
            if s < 3 or (s == 3 and direction == 0):
                go(zmove1(direction, s))
            spread(k)

        return run

    def xstep1(k, direction):
        def run():
            xmove(direction, k)().wait_recv()
            xj = (xa + NX - 1) % NX if direction == 0 else (xa + 1) % NX
            if k % 2 == direction:
                go(xforward(k))
            sibling(piece1(xj, zslot(*hops[k])))

        return run

    def fstep1(k):
        def run():
            xforward(k)().wait_recv()
            sibling(piece1((xa + 2) % NX, zslot(*hops[k])))

        return run

    todo1 = [lambda: begin1(own_w), lambda: begin1(own_p), first1]
    for k in range(1, 8):
        todo1.append(zstep1(k))
        if k >= 3:
            todo1 += [xstep1(k - 3, 0), xstep1(k - 3, 1)]
        if k >= 6:
            todo1.append(fstep1(k - 6))
    for k in (5, 6, 7):
        todo1 += [xstep1(k, 0), xstep1(k, 1), fstep1(k - 3)]
    todo1 += [fstep1(k) for k in (5, 6, 7)]

    def advance(n0, n1):
        head0, head1 = todo0[:n0], todo1[:n1]
        del todo0[:n0], todo1[:n1]
        if head0:
            @pl.when(core == 0)
            def _():
                for run in head0:
                    run()
        if head1:
            @pl.when(core == 1)
            def _():
                for run in head1:
                    run()

    p_slab = f // 32
    p_row = f % 32
    p_src = pgt.at[p_row]

    @pl.when(p_slab == t)
    def _():
        def send(d):
            copy(p_src, own_p, ps, pr, {"tp": peer_t(d)}).start()

        each(1, NT, send)
        wfull[yl, xa, z, core, :, HIDL:HIDP] = pgt[p_row]

    advance(1, 1)

    @pl.when(carries)
    def _():
        def send(d):
            q, dev = peer_p(d)
            copy(s1src.at[q], s1dst.at[p], s1ss, s1rs, {"fsdp": dev}).start()

        each(1, NP, send)
        s1dst[p] = s1src[p]

    xv = xfull[t].reshape(256, 512)
    pu = lax.dot_general(xv, pg_hi, NT_DIMS, preferred_element_type=F32)
    pu = pu + lax.dot_general(xv, pg_lo, NT_DIMS, preferred_element_type=F32)
    xv = xv.astype(F32)
    sq_hi, sq_lo = split_hi_lo(jnp.sum(xv * xv, axis=1, keepdims=True))
    sq2 = jnp.where(iota((256, 128), 1) < 64, sq_hi, sq_lo)
    usend[:, :, 0:128] = pu.astype(BF).reshape(4, 64, 128)
    usend[:, :, 128:256] = sq2.astype(BF).reshape(4, 64, 128)

    def send_u(d):
        q = peer_t(d)
        copy(usend.at[q], urecv.at[t], us, ur, {"tp": q}).start()

    each(1, NT, send_u)
    urecv[t] = usend[t]

    tdev = ({"tp": (t + 1) % NT}, {"tp": (t + NT - 1) % NT})

    def x_move(direction, h):
        part = xfull.at[t, h]
        return copy(part, part, dhs, dhr.at[direction, h], tdev[direction])

    def x_forward(direction):
        part = xfull.at[(t + NT - 1) % NT if direction == 0 else (t + 1) % NT, direction]
        return copy(part, part, dhs, dfr.at[direction], tdev[direction])

    @pl.when(p_slab != t)
    def _():
        copy(p_src, own_p, ps, pr, tdev[0]).wait_recv()

    advance(2, 1)

    slot = grp % 2

    @pl.when(carries)
    def _():
        copy(s1src.at[0:15], s1dst.at[0:15], s1ss, s1rs, near_p).wait_recv()
        rows = permute_rows(
            256,
            lambda r: ((r >> 1) & 15) * 16 + (r >> 5) * 2 + (r & 1),
            s1dst[...].reshape(256, 128),
        )
        s2src[...] = rows.astype(BF).reshape(8, 32, 128)

        def send(d):
            q, dev = peer_g(d)
            copy(s2src.at[q], s2dst.at[slot], s2ss, s2rs.at[slot], {"fsdp": dev}).start()

        each(1, NG, send)
        s2dst[slot] = s2src[grp]

    advance(4, 1)
    for direction in (0, 1):
        x_move(direction, direction).start()

    copy(usend.at[0:3], urecv.at[0:3], us, ur, tdev[0]).wait_recv()
    summed = jnp.sum(urecv[...].astype(F32), axis=0)
    u = summed[:, 0:128]
    lane = iota((64, 128), 1)
    sq = jnp.sum(
        jnp.where((lane == 0) | (lane == 64), summed[:, 128:256], 0.0), axis=1, keepdims=True
    )
    inv = lax.rsqrt(sq / D + 1e-06)
    zvals = inv * u + b_ref[...]
    kinv = lax.rsqrt(jnp.sum(zvals * zvals, axis=1, keepdims=True) + 1e-06)
    emb = zvals * kinv
    advance(0, 1)

    for i in range(2):
        @pl.when(jnp.logical_not(carries & (slot == i)))
        def _(i=i):
            copy(s2src.at[0], s2dst.at[i], s2ss, s2rs.at[i], {"fsdp": peer_g(1)[1]}).wait_recv()

    position = core * 256 + t * 64 + iota((64, 128), 0)
    grads = jnp.where(
        position < len_ref[f // 2], s2dst[...].reshape(64, 128).astype(F32), 0.0
    )
    dz = kinv * (grads - emb * jnp.sum(emb * grads, axis=1, keepdims=True))
    cvals = jnp.sum(dz * u, axis=1, keepdims=True)
    coef = inv * inv * inv * cvals / D
    inv_hi, inv_lo = split_hi_lo(inv)
    coef_hi, coef_lo = split_hi_lo(coef)
    tail = jnp.where(
        lane < 64,
        jnp.where(lane < 32, inv_hi, inv_lo),
        jnp.where(lane < 96, coef_hi, coef_lo),
    )
    dzfull[t, :, 0:128] = dz.astype(BF)
    dzfull[t, :, 128:256] = tail.astype(BF)

    def send_dz(d):
        part = dzfull.at[t]
        copy(part, part, ds, dr, {"tp": peer_t(d)}).start()

    each(1, NT, send_dz)
    advance(11, 4)

    copy(dzfull.at[0:3], dzfull.at[0:3], ds, dr, tdev[0]).wait_recv()
    for direction in (0, 1):
        x_move(direction, 1 - direction).start()
    dzall = dzfull[:, :, 0:128].reshape(256, 128)
    tails = dzfull[:, :, 128:256].reshape(256, 128).astype(F32)
    lane = iota((256, 128), 1)
    inv = jnp.sum(jnp.where((lane == 0) | (lane == 32), tails, 0.0), axis=1, keepdims=True)
    coef = jnp.sum(jnp.where((lane == 64) | (lane == 96), tails, 0.0), axis=1, keepdims=True)
    dzf = dzall.astype(F32)
    xinv = (xfull[t].reshape(256, 512).astype(F32) * (inv * (1.0 / 64.0))).astype(BF)
    sums = jnp.dot(dzf.T.astype(BF), xinv, preferred_element_type=F32)
    bsum = jnp.sum(dzf, axis=0, keepdims=True) * (1.0 / 64.0)
    row8 = iota((8, 128), 0)
    extra = jnp.where(row8 == 0, bsum, 0.0)

    def pack_extra(value):
        hi, lo = split_hi_lo(value)
        return jnp.concatenate([hi, lo], axis=0).astype(BF)

    main = jnp.concatenate(
        [sums[:, 0:256].reshape(16, 8, 256), sums[:, 256:512].reshape(16, 8, 256)], axis=1
    )
    rs_src[:, :, 0:256] = main.astype(BF)
    rs_src[:, :, 256:384] = jnp.broadcast_to(pack_extra(extra)[None], (16, 16, 128))

    def send_rs(d):
        q, dev = peer_p(d)
        copy(rs_src.at[q], rs_dst.at[p], rss, rsr, {"fsdp": dev}).start()

    each(1, NP, send_rs)
    rs_dst[p] = rs_src[p]
    advance(8, 7)
    for direction in (0, 1):
        x_move(direction, direction).wait_recv()
        x_forward(direction).start()
    advance(4, 5)

    copy(rs_src.at[0:15], rs_dst.at[0:15], rss, rsr, near_p).wait_recv()
    part = jnp.sum(rs_dst[...].astype(F32), axis=0)
    zbuf[grp, :, 0:256] = part[:, 0:256].astype(BF)
    zbuf[grp, :, 256:384] = pack_extra(part[0:8, 256:384] + part[8:16, 256:384])

    def send_z(d):
        q, dev = peer_g(d)
        copy(zbuf.at[grp], zbuf.at[grp], zss, zsr, {"fsdp": dev}).start()

    each(1, NG, send_z)
    advance(4, 12)
    copy(zbuf.at[0:7], zbuf.at[0:7], zss, zsr, near_g).wait_recv()
    part = jnp.sum(zbuf[...].astype(F32), axis=0)
    ag[p] = part[:, 0:256].astype(BF)
    bias_ref[...] = (part[0:8, 256:384] + part[8:16, 256:384])[0:1]

    def send_ag(d):
        q, dev = peer_p(d)
        copy(ag.at[p], ag.at[p], ags, agr, {"fsdp": dev}).start()

    each(1, NP, send_ag)
    advance(len(todo0), len(todo1))

    for direction in (0, 1):
        x_move(direction, 1 - direction).wait_recv()
        x_forward(direction).wait_recv()
    copy(wfull.at[:, :, :, core], wfull.at[:, :, :, 1 - core], sibs, sibr, {"fsdp": f + 1 - 2 * core}).wait()
    for j in range(NT):
        for k in range(2):
            pgt_part = wfull[j // 2, (j % 2) * 2 + k, :, :, :, HIDL:HIDP].reshape(256, 128)
            dn = lax.dot_general(dzall, pgt_part, NT_DIMS, preferred_element_type=F32)
            xpart = xfull[j, :, :, k * 256 : k * 256 + 256].reshape(256, 256).astype(F32)
            lo = j * 512 + k * 256
            dhv[:, lo : lo + 256] = (inv * dn - xpart * coef).astype(BF)
    stores = []

    def store(src, dst):
        move = pltpu.make_async_copy(src, dst, outs.at[len(stores)])
        move.start()
        stores.append(move)

    store(bias_ref, bias_out)
    for lo, hi in ((0, 512), (512, 1024), (1024, 1408)):
        act_ref[:, lo:hi] = jnp.dot(
            dhv[...], wfull[:, :, :, :, :, lo:hi].reshape(D, hi - lo), preferred_element_type=F32
        ).astype(BF)
        store(act_ref.at[:, lo:hi], act_out.at[:, lo:hi])

    copy(rs_src.at[0:15], rs_dst.at[0:15], rss, rsr, near_p).wait_send()
    copy(zbuf.at[0:7], zbuf.at[0:7], zss, zsr, near_g).wait_send()
    copy(usend.at[0:3], urecv.at[0:3], us, ur, tdev[0]).wait_send()
    copy(dzfull.at[0:3], dzfull.at[0:3], ds, dr, tdev[0]).wait_send()
    copy(xfull.at[0:3], xfull.at[0:3], dhs, dfr.at[0], tdev[0]).wait_send()

    @pl.when(p_slab == t)
    def _():
        copy(pgt.at[0:3], pgt.at[0:3], ps, pr, tdev[0]).wait_send()

    @pl.when(carries)
    def _():
        copy(s1src.at[0:15], s1dst.at[0:15], s1ss, s1rs, near_p).wait_send()
        copy(s2src.at[0:7], s2src.at[0:7], s2ss, s2rs.at[0], near_g).wait_send()

    def all_left(part, send_sem):
        copy(part, part, send_sem, wr.at[0], zdev[0]).wait_send()

    @pl.when(core == 0)
    def _():
        all_left(wfull.at[:, :, 0:7, 0], ringsend)
        all_left(wfull.at[0, 0, 0:7, 0], sidesend)

    @pl.when(core == 1)
    def _():
        all_left(wfull.at[0, 0:3, 0:5, 1], ringsend)
        all_left(wfull.at[:, 0:3, :, 1], sidesend)

    copy(ag.at[0:15], ag.at[0:15], ags, agr, near_p).wait()
    full = ag[...].astype(F32)
    full = jnp.concatenate(
        [full[:, 0:8].reshape(128, 256), full[:, 8:16].reshape(128, 256)], axis=1
    )
    proj_ref[...] = full * gain
    gain_ref[...] = jnp.sum(full * p_ref[...], axis=0, keepdims=True)
    store(proj_ref, proj_out)
    store(gain_ref, gain_out)

    for move in stores:
        move.wait()


def shards(token_grads, hidden, proj_weight, proj_bias, norm_gain, down_weight, lengths):
    sem = pltpu.SemaphoreType.DMA
    anywhere = pl.BlockSpec(memory_space=pl.ANY)
    results = (
        jax.ShapeDtypeStruct((256, HIDL), BF),
        jax.ShapeDtypeStruct((128, 512), F32),
        jax.ShapeDtypeStruct((1, 512), F32),
        jax.ShapeDtypeStruct((1, 128), F32),
    )
    act, proj, gain, bias = pl.pallas_call(
        kernel,
        out_shape=results,
        in_specs=[anywhere] * 7,
        out_specs=(anywhere,) * 4,
        scratch_shapes=[
            pltpu.VMEM((256, HIDL), BF),
            pltpu.VMEM((128, 512), F32),
            pltpu.VMEM((1, 512), F32),
            pltpu.VMEM((1, 128), F32),
            sem((6,)),
            pltpu.VMEM((256, 128), F32),
            pltpu.VMEM((NT, 2, 128, 512), BF),
            pltpu.VMEM((128, 512), F32),
            pltpu.VMEM((1, 128), F32),
            pltpu.VMEM((1, 512), F32),
            pltpu.VMEM((16, HIDL), F32),
            pltpu.SMEM((64,), I32),
            pltpu.VMEM((2, NX, NZ, 2, 16, HIDP), BF),
            pltpu.VMEM((32, 16, 128), BF),
            pltpu.VMEM((NT, 64, 256), BF),
            pltpu.VMEM((NT, 64, 256), BF),
            pltpu.VMEM((NP, 16, 128), BF),
            pltpu.VMEM((NP, 16, 128), BF),
            pltpu.VMEM((NG, 32, 128), BF),
            pltpu.VMEM((2, 32, 128), BF),
            pltpu.VMEM((NT, 64, 256), BF),
            pltpu.VMEM((256, D), BF),
            pltpu.VMEM((NP, 16, 384), BF),
            pltpu.VMEM((NP, 16, 384), BF),
            pltpu.VMEM((NG, 16, 384), BF),
            pltpu.VMEM((NP, 16, 256), BF),
            sem((7,)),
            sem, sem, sem((64,)), sem, sem,
            sem, sem, sem, sem((2,)),
            sem, sem, sem, sem,
            sem, sem,
            sem, sem((2, 2)), sem((2,)),
            sem, sem, sem, sem, sem, sem,
        ],
        compiler_params=pltpu.CompilerParams(
            collective_id=0, has_side_effects=True, vmem_limit_bytes=VLIM
        ),
    )(
        token_grads, hidden.reshape(2, 128, 512), proj_weight, proj_bias.reshape(1, 128),
        norm_gain.reshape(1, 512), down_weight.T, lengths,
    )
    return act, proj, gain.reshape(512), bias.reshape(128)


def solution(mesh):
    placed = (P("fsdp", None), P("fsdp", "tp"), P(None, "tp"), P(), P("tp"), P("tp", "fsdp"), P())
    return jax.shard_map(
        shards,
        mesh=mesh,
        in_specs=placed,
        out_specs=(P("fsdp", "tp"), P(None, "tp"), P("tp"), P()),
        check_vma=False,
    )
```

```python
import jax
import jax.numpy as jnp
from jax import lax
from jax.experimental import pallas as pl
from jax.experimental.pallas import tpu as pltpu
from jax.sharding import PartitionSpec as P

D = 2048
LEN = 512
NX, NZ, NG, NP, NT = 4, 8, 8, 16, 4
HIDL, HIDP = 1408, 1536
YREC, XREC = 28, {1: 29, 2: 30, 3: 31, 5: 56, 6: 57, 7: 58}
VLIM = 56 * 1024 * 1024
MESH = pl.DeviceIdType.MESH
HIGH = lax.Precision.HIGHEST
BF, F32, I32 = jnp.bfloat16, jnp.float32, jnp.int32
NT_DIMS = (((1,), (1,)), ((), ()))


def iota(shape, axis):
    return lax.broadcasted_iota(I32, shape, axis)


def split_hi_lo(value):
    hi = value.astype(BF).astype(F32)
    return hi, value - hi


def permute_rows(count, source_of, rows):
    hot = jnp.where(
        iota((count, count), 1) == source_of(iota((count, count), 0)), F32(1.0), F32(0.0)
    ).astype(BF)
    return jnp.dot(hot, rows, preferred_element_type=F32)


def kernel(
    tg_hbm, x_hbm, p_hbm, b_hbm, g_hbm, w_hbm, len_hbm,
    act_out, proj_out, gain_out, bias_out,
    act_ref, proj_ref, gain_ref, bias_ref, outs,
    tg_ref, xfull, p_ref, b_ref, g_ref, w_ref, len_ref,
    wfull, pgt, usend, urecv, s1src, s1dst, s2src, s2dst, dzfull, dhv, rs_src, rs_dst, zbuf, ag,
    ins, ringsend, sidesend, wr, sibs, sibr,
    s1ss, s1rs, s2ss, s2rs, us, ur, ps, pr, ds, dr, dhs, dhr, dfr, rss, rsr, zss, zsr, ags, agr,
):
    f = lax.axis_index("fsdp")
    t = lax.axis_index("tp")
    core = f % 2
    z = (f // 2) % NZ
    grp = f // 16
    xa = grp % NX
    yl = grp // NX
    p = f % 16

    def at_f(group, zpos, cpos):
        return group * 16 + zpos * 2 + cpos

    def peer_p(d):
        q = (p + d) % NP
        return q, grp * 16 + q

    def peer_g(d):
        q = (grp + d) % NG
        return q, q * 16 + p

    def peer_t(d):
        return (t + d) % NT

    def copy(src, dst, ssem, rsem, dev):
        return pltpu.make_async_remote_copy(
            src_ref=src, dst_ref=dst, send_sem=ssem, recv_sem=rsem,
            device_id=dev, device_id_type=MESH,
        )

    def each(lo, hi, body):
        def step(d, carry):
            body(d)
            return carry

        lax.fori_loop(lo, hi, step, 0)

    loads = [
        pltpu.make_async_copy(src, dst, ins.at[i])
        for i, (src, dst) in enumerate((
            (w_hbm, w_ref), (tg_hbm, tg_ref), (x_hbm, xfull.at[t]), (p_hbm, p_ref),
            (g_hbm, g_ref), (b_hbm, b_ref), (len_hbm, len_ref),
        ))
    ]
    for load in loads:
        load.start()

    near_p = {"fsdp": peer_p(1)[1]}
    near_g = {"fsdp": peer_g(1)[1]}

    bar = pltpu.get_barrier_semaphore()

    def greet(dev):
        pl.semaphore_signal(bar, inc=1, device_id=dev, device_id_type=MESH)

    each(1, NP, lambda d: greet({"fsdp": peer_p(d)[1]}))
    each(1, NG, lambda d: greet({"fsdp": peer_g(d)[1]}))
    each(1, NT, lambda d: greet({"tp": peer_t(d)}))

    loads[0].wait()
    wfull[yl, xa, z, core, :, 0:HIDL] = w_ref[...].astype(BF)
    loads[1].wait()
    carries = grp // 2 == t

    @pl.when(carries)
    def _():
        rows = permute_rows(
            256, lambda r: ((r >> 1) & 7) * 32 + (r >> 4) * 2 + (r & 1), tg_ref[...].astype(BF)
        )
        s1src[...] = rows.astype(BF).reshape(16, 16, 128)

    for load in loads[2:]:
        load.wait()
    gain = g_ref[...]
    pg = p_ref[...] * gain
    pg_hi = pg.astype(BF)
    pg_lo = (pg - pg_hi.astype(F32)).astype(BF)
    pgt[...] = pg.T.astype(BF).reshape(32, 16, 128)
    pl.semaphore_wait(bar, (NP - 1) + (NG - 1) + (NT - 1))

    def go(make):
        make().start()

    def sibling(piece):
        copy(piece, piece, sibs, sibr, {"fsdp": f + 1 - 2 * core}).start()

    own = wfull.at[yl, xa, z, core]
    met = wfull.at[1 - yl, xa, z, core]
    met_w = wfull.at[1 - yl, xa, z, core, :, pl.ds(0, HIDL)]
    met_p = wfull.at[1 - yl, xa, z, core, :, pl.ds(HIDL, 128)]
    own_w = wfull.at[yl, xa, z, core, :, pl.ds(0, HIDL)]
    own_p = wfull.at[yl, xa, z, core, :, pl.ds(HIDL, 128)]
    zdev = ({"fsdp": at_f(grp, (z + 1) % NZ, core)}, {"fsdp": at_f(grp, (z + NZ - 1) % NZ, core)})
    xdev = (
        {"fsdp": at_f(yl * NX + (xa + 1) % NX, z, core)},
        {"fsdp": at_f(yl * NX + (xa + NX - 1) % NX, z, core)},
    )

    ydev = {"fsdp": at_f((grp + NX) % NG, z, core)}

    def zslot(direction, s):
        return (z + NZ - s) % NZ if direction == 0 else (z + s) % NZ

    def piece0(i, zj):
        return wfull.at[yl if i < NX else 1 - yl, (xa + i % NX) % NX, zj, 0]

    def xdev_at(d):
        return {"fsdp": at_f(yl * NX + (xa + d) % NX, z, core)}

    def zmove0(direction, s, i):
        def make():
            piece = piece0(i, zslot(direction, s))
            return copy(piece, piece, ringsend, wr.at[direction * 32 + s * 8 + i], zdev[direction])

        return make

    def launch0(i):
        for direction in (0, 1):
            go(zmove0(direction, 0, i))
        sibling(piece0(i, z))

    def begin0(part, yrec):
        go(lambda: copy(part, part, sidesend, wr.at[yrec], ydev))
        for d in range(1, NX):
            go(lambda d=d: copy(part, part, sidesend, wr.at[XREC[d]], xdev_at(NX - d)))
        for direction in (0, 1):
            go(lambda: copy(part, part, ringsend, wr.at[direction * 32], zdev[direction]))

    def end_begin0():
        begin0(own_p, YREC + 31)
        sibling(own)

    def relay0(part, yrec):
        copy(part, part, sidesend, wr.at[yrec], ydev).wait_recv()
        for d in range(1, NX):
            go(lambda d=d: copy(part, part, sidesend, wr.at[XREC[NX + d]], xdev_at(NX - d)))
        for direction in (0, 1):
            go(lambda: copy(part, part, ringsend, wr.at[direction * 32 + NX], zdev[direction]))

    def end_relay0():
        relay0(met_p, YREC + 31)
        sibling(met)

    def ring0(i):
        def run():
            copy(own, own, sidesend, wr.at[XREC[i]], zdev[0]).wait_recv()
            launch0(i)

        return run

    def arrive0(s, direction, i):
        zmove0(direction, s - 1, i)().wait_recv()
        if s < 3 or (s == 3 and (i < NX) == (direction == 0)):
            go(zmove0(direction, s, i))
        sibling(piece0(i, zslot(direction, s)))

    def step0(s, i):
        def run():
            if s < 4 or i < NX:
                arrive0(s, 0, i)
            if s < 4:
                arrive0(s, 1, i)
            elif i < NX:
                arrive0(s, 1, i + NX)

        return run

    todo0 = [lambda: begin0(own_w, YREC), end_begin0, lambda: relay0(met_w, YREC)]
    todo0 += [ring0(1), ring0(3), ring0(2), end_relay0, step0(1, 0), ring0(5), ring0(7), ring0(6)]
    order = (1, 3, 2, 4, 5, 7, 6)
    todo0 += [step0(1, i) for i in order]
    todo0 += [step0(2, i) for i in (0,) + order] + [step0(3, i) for i in (0,) + order]
    todo0 += [step0(4, i) for i in (0, 1, 3, 2)]

    hops = [(0, 0), (0, 1), (1, 1), (0, 2), (1, 2), (0, 3), (1, 3), (0, 4)]

    def piece1(xj, zj):
        return wfull.at[:, xj, zj, 1]

    def zmove1(direction, s):
        def make():
            piece = piece1(xa, zslot(direction, s))
            return copy(piece, piece, ringsend, wr.at[direction * 4 + s], zdev[direction])

        return make

    def xmove(direction, k):
        def make():
            piece = piece1(xa, zslot(*hops[k]))
            return copy(piece, piece, sidesend, wr.at[8 + direction * 8 + k], xdev[direction])

        return make

    def xforward(k):
        direction = k % 2

        def make():
            xj = (xa + NX - 1) % NX if direction == 0 else (xa + 1) % NX
            piece = piece1(xj, zslot(*hops[k]))
            return copy(piece, piece, sidesend, wr.at[24 + k], xdev[direction])

        return make

    def begin1(part):
        go(lambda: copy(part, part, ringsend, wr.at[32], ydev))

    def spread(k):
        go(xmove(0, k))
        go(xmove(1, k))
        sibling(piece1(xa, zslot(*hops[k])))

    def first1():
        copy(met, met, ringsend, wr.at[32], ydev).wait_recv()
        go(zmove1(0, 0))
        go(zmove1(1, 0))
        spread(0)

    def zstep1(k):
        def run():
            direction, s = hops[k]
            zmove1(direction, s - 1)().wait_recv()
            if s < 3 or (s == 3 and direction == 0):
                go(zmove1(direction, s))
            spread(k)

        return run

    def xstep1(k, direction):
        def run():
            xmove(direction, k)().wait_recv()
            xj = (xa + NX - 1) % NX if direction == 0 else (xa + 1) % NX
            if k % 2 == direction:
                go(xforward(k))
            sibling(piece1(xj, zslot(*hops[k])))

        return run

    def fstep1(k):
        def run():
            xforward(k)().wait_recv()
            sibling(piece1((xa + 2) % NX, zslot(*hops[k])))

        return run

    todo1 = [lambda: begin1(own_w), lambda: begin1(own_p), first1]
    for k in range(1, 8):
        todo1.append(zstep1(k))
        if k >= 3:
            todo1 += [xstep1(k - 3, 0), xstep1(k - 3, 1)]
        if k >= 6:
            todo1.append(fstep1(k - 6))
    for k in (5, 6, 7):
        todo1 += [xstep1(k, 0), xstep1(k, 1), fstep1(k - 3)]
    todo1 += [fstep1(k) for k in (5, 6, 7)]

    def advance(n0, n1):
        head0, head1 = todo0[:n0], todo1[:n1]
        del todo0[:n0], todo1[:n1]
        if head0:
            @pl.when(core == 0)
            def _():
                for run in head0:
                    run()
        if head1:
            @pl.when(core == 1)
            def _():
                for run in head1:
                    run()

    p_slab = f // 32
    p_row = f % 32
    p_src = pgt.at[p_row]

    @pl.when(p_slab == t)
    def _():
        def send(d):
            copy(p_src, own_p, ps, pr, {"tp": peer_t(d)}).start()

        each(1, NT, send)
        wfull[yl, xa, z, core, :, HIDL:HIDP] = pgt[p_row]

    @pl.when(carries)
    def _():
        def send(d):
            q, dev = peer_p(d)
            copy(s1src.at[q], s1dst.at[p], s1ss, s1rs, {"fsdp": dev}).start()

        each(1, NP, send)
        s1dst[p] = s1src[p]

    advance(1, 1)

    xv = xfull[t].reshape(256, 512)
    pu = lax.dot_general(xv, pg_hi, NT_DIMS, preferred_element_type=F32)
    pu = pu + lax.dot_general(xv, pg_lo, NT_DIMS, preferred_element_type=F32)
    xv = xv.astype(F32)
    sq_hi, sq_lo = split_hi_lo(jnp.sum(xv * xv, axis=1, keepdims=True))
    sq2 = jnp.where(iota((256, 128), 1) < 64, sq_hi, sq_lo)
    usend[:, :, 0:128] = pu.astype(BF).reshape(4, 64, 128)
    usend[:, :, 128:256] = sq2.astype(BF).reshape(4, 64, 128)

    def send_u(d):
        q = peer_t(d)
        copy(usend.at[q], urecv.at[t], us, ur, {"tp": q}).start()

    each(1, NT, send_u)
    urecv[t] = usend[t]

    tdev = ({"tp": (t + 1) % NT}, {"tp": (t + NT - 1) % NT})

    def x_move(direction, h):
        part = xfull.at[t, h]
        return copy(part, part, dhs, dhr.at[direction, h], tdev[direction])

    def x_forward(direction):
        part = xfull.at[(t + NT - 1) % NT if direction == 0 else (t + 1) % NT, direction]
        return copy(part, part, dhs, dfr.at[direction], tdev[direction])

    @pl.when(p_slab != t)
    def _():
        copy(p_src, own_p, ps, pr, tdev[0]).wait_recv()

    advance(2, 1)

    slot = grp % 2

    @pl.when(carries)
    def _():
        copy(s1src.at[0:15], s1dst.at[0:15], s1ss, s1rs, near_p).wait_recv()
        rows = permute_rows(
            256,
            lambda r: ((r >> 1) & 15) * 16 + (r >> 5) * 2 + (r & 1),
            s1dst[...].reshape(256, 128),
        )
        s2src[...] = rows.astype(BF).reshape(8, 32, 128)

        def send(d):
            q, dev = peer_g(d)
            copy(s2src.at[q], s2dst.at[slot], s2ss, s2rs.at[slot], {"fsdp": dev}).start()

        each(1, NG, send)
        s2dst[slot] = s2src[grp]

    advance(4, 1)

    copy(usend.at[0:3], urecv.at[0:3], us, ur, tdev[0]).wait_recv()
    summed = jnp.sum(urecv[...].astype(F32), axis=0)
    u = summed[:, 0:128]
    lane = iota((64, 128), 1)
    sq = jnp.sum(
        jnp.where((lane == 0) | (lane == 64), summed[:, 128:256], 0.0), axis=1, keepdims=True
    )
    inv = lax.rsqrt(sq / D + 1e-06)
    zvals = inv * u + b_ref[...]
    kinv = lax.rsqrt(jnp.sum(zvals * zvals, axis=1, keepdims=True) + 1e-06)
    emb = zvals * kinv
    advance(0, 1)

    for i in range(2):
        @pl.when(jnp.logical_not(carries & (slot == i)))
        def _(i=i):
            copy(s2src.at[0], s2dst.at[i], s2ss, s2rs.at[i], {"fsdp": peer_g(1)[1]}).wait_recv()

    position = core * 256 + t * 64 + iota((64, 128), 0)
    grads = jnp.where(
        position < len_ref[f // 2], s2dst[...].reshape(64, 128).astype(F32), 0.0
    )
    dz = kinv * (grads - emb * jnp.sum(emb * grads, axis=1, keepdims=True))
    cvals = jnp.sum(dz * u, axis=1, keepdims=True)
    coef = inv * inv * inv * cvals / D
    inv_hi, inv_lo = split_hi_lo(inv)
    coef_hi, coef_lo = split_hi_lo(coef)
    tail = jnp.where(
        lane < 64,
        jnp.where(lane < 32, inv_hi, inv_lo),
        jnp.where(lane < 96, coef_hi, coef_lo),
    )
    dzfull[t, :, 0:128] = dz.astype(BF)
    dzfull[t, :, 128:256] = tail.astype(BF)

    def send_dz(d):
        part = dzfull.at[t]
        copy(part, part, ds, dr, {"tp": peer_t(d)}).start()

    each(1, NT, send_dz)
    for direction in (0, 1):
        x_move(direction, direction).start()
    advance(8, 3)

    copy(dzfull.at[0:3], dzfull.at[0:3], ds, dr, tdev[0]).wait_recv()
    for direction in (0, 1):
        x_move(direction, 1 - direction).start()
    dzall = dzfull[:, :, 0:128].reshape(256, 128)
    tails = dzfull[:, :, 128:256].reshape(256, 128).astype(F32)
    lane = iota((256, 128), 1)
    inv = jnp.sum(jnp.where((lane == 0) | (lane == 32), tails, 0.0), axis=1, keepdims=True)
    coef = jnp.sum(jnp.where((lane == 64) | (lane == 96), tails, 0.0), axis=1, keepdims=True)
    dzf = dzall.astype(F32)
    xinv = (xfull[t].reshape(256, 512).astype(F32) * (inv * (1.0 / 64.0))).astype(BF)
    sums = jnp.dot(dzf.T.astype(BF), xinv, preferred_element_type=F32)
    bsum = jnp.sum(dzf, axis=0, keepdims=True) * (1.0 / 64.0)
    row8 = iota((8, 128), 0)
    extra = jnp.where(row8 == 0, bsum, 0.0)

    def pack_extra(value):
        hi, lo = split_hi_lo(value)
        return jnp.concatenate([hi, lo], axis=0).astype(BF)

    main = jnp.concatenate(
        [sums[:, 0:256].reshape(16, 8, 256), sums[:, 256:512].reshape(16, 8, 256)], axis=1
    )
    rs_src[:, :, 0:256] = main.astype(BF)
    rs_src[:, :, 256:384] = jnp.broadcast_to(pack_extra(extra)[None], (16, 16, 128))

    def send_rs(d):
        q, dev = peer_p(d)
        copy(rs_src.at[q], rs_dst.at[p], rss, rsr, {"fsdp": dev}).start()

    each(1, NP, send_rs)
    rs_dst[p] = rs_src[p]
    advance(10, 9)

    copy(rs_src.at[0:15], rs_dst.at[0:15], rss, rsr, near_p).wait_recv()
    part = jnp.sum(rs_dst[...].astype(F32), axis=0)
    zbuf[grp, :, 0:256] = part[:, 0:256].astype(BF)
    zbuf[grp, :, 256:384] = pack_extra(part[0:8, 256:384] + part[8:16, 256:384])

    def send_z(d):
        q, dev = peer_g(d)
        copy(zbuf.at[grp], zbuf.at[grp], zss, zsr, {"fsdp": dev}).start()

    each(1, NG, send_z)
    for direction in (0, 1):
        x_move(direction, direction).wait_recv()
        x_forward(direction).start()
    advance(9, 13)
    copy(zbuf.at[0:7], zbuf.at[0:7], zss, zsr, near_g).wait_recv()
    part = jnp.sum(zbuf[...].astype(F32), axis=0)
    ag[p] = part[:, 0:256].astype(BF)
    bias_ref[...] = (part[0:8, 256:384] + part[8:16, 256:384])[0:1]

    def send_ag(d):
        q, dev = peer_p(d)
        copy(ag.at[p], ag.at[p], ags, agr, {"fsdp": dev}).start()

    each(1, NP, send_ag)
    advance(len(todo0), len(todo1))

    for direction in (0, 1):
        x_move(direction, 1 - direction).wait_recv()
        x_forward(direction).wait_recv()
    copy(wfull.at[:, :, :, core], wfull.at[:, :, :, 1 - core], sibs, sibr, {"fsdp": f + 1 - 2 * core}).wait()
    for j in range(NT):
        for k in range(2):
            pgt_part = wfull[j // 2, (j % 2) * 2 + k, :, :, :, HIDL:HIDP].reshape(256, 128)
            dn = lax.dot_general(dzall, pgt_part, NT_DIMS, preferred_element_type=F32)
            xpart = xfull[j, :, :, k * 256 : k * 256 + 256].reshape(256, 256).astype(F32)
            lo = j * 512 + k * 256
            dhv[:, lo : lo + 256] = (inv * dn - xpart * coef).astype(BF)
    stores = []

    def store(src, dst):
        move = pltpu.make_async_copy(src, dst, outs.at[len(stores)])
        move.start()
        stores.append(move)

    store(bias_ref, bias_out)
    for lo, hi in ((0, 512), (512, 1024), (1024, 1408)):
        act_ref[:, lo:hi] = jnp.dot(
            dhv[...], wfull[:, :, :, :, :, lo:hi].reshape(D, hi - lo), preferred_element_type=F32
        ).astype(BF)
        store(act_ref.at[:, lo:hi], act_out.at[:, lo:hi])

    copy(rs_src.at[0:15], rs_dst.at[0:15], rss, rsr, near_p).wait_send()
    copy(zbuf.at[0:7], zbuf.at[0:7], zss, zsr, near_g).wait_send()
    copy(usend.at[0:3], urecv.at[0:3], us, ur, tdev[0]).wait_send()
    copy(dzfull.at[0:3], dzfull.at[0:3], ds, dr, tdev[0]).wait_send()
    copy(xfull.at[0:3], xfull.at[0:3], dhs, dfr.at[0], tdev[0]).wait_send()

    @pl.when(p_slab == t)
    def _():
        copy(pgt.at[0:3], pgt.at[0:3], ps, pr, tdev[0]).wait_send()

    @pl.when(carries)
    def _():
        copy(s1src.at[0:15], s1dst.at[0:15], s1ss, s1rs, near_p).wait_send()
        copy(s2src.at[0:7], s2src.at[0:7], s2ss, s2rs.at[0], near_g).wait_send()

    def all_left(part, send_sem):
        copy(part, part, send_sem, wr.at[0], zdev[0]).wait_send()

    @pl.when(core == 0)
    def _():
        all_left(wfull.at[:, :, 0:7, 0], ringsend)
        all_left(wfull.at[0, 0, 0:7, 0], sidesend)

    @pl.when(core == 1)
    def _():
        all_left(wfull.at[0, 0:3, 0:5, 1], ringsend)
        all_left(wfull.at[:, 0:3, :, 1], sidesend)

    copy(ag.at[0:15], ag.at[0:15], ags, agr, near_p).wait()
    full = ag[...].astype(F32)
    full = jnp.concatenate(
        [full[:, 0:8].reshape(128, 256), full[:, 8:16].reshape(128, 256)], axis=1
    )
    proj_ref[...] = full * gain
    gain_ref[...] = jnp.sum(full * p_ref[...], axis=0, keepdims=True)
    store(proj_ref, proj_out)
    store(gain_ref, gain_out)

    for move in stores:
        move.wait()


def shards(token_grads, hidden, proj_weight, proj_bias, norm_gain, down_weight, lengths):
    sem = pltpu.SemaphoreType.DMA
    anywhere = pl.BlockSpec(memory_space=pl.ANY)
    results = (
        jax.ShapeDtypeStruct((256, HIDL), BF),
        jax.ShapeDtypeStruct((128, 512), F32),
        jax.ShapeDtypeStruct((1, 512), F32),
        jax.ShapeDtypeStruct((1, 128), F32),
    )
    act, proj, gain, bias = pl.pallas_call(
        kernel,
        out_shape=results,
        in_specs=[anywhere] * 7,
        out_specs=(anywhere,) * 4,
        scratch_shapes=[
            pltpu.VMEM((256, HIDL), BF),
            pltpu.VMEM((128, 512), F32),
            pltpu.VMEM((1, 512), F32),
            pltpu.VMEM((1, 128), F32),
            sem((6,)),
            pltpu.VMEM((256, 128), F32),
            pltpu.VMEM((NT, 2, 128, 512), BF),
            pltpu.VMEM((128, 512), F32),
            pltpu.VMEM((1, 128), F32),
            pltpu.VMEM((1, 512), F32),
            pltpu.VMEM((16, HIDL), F32),
            pltpu.SMEM((64,), I32),
            pltpu.VMEM((2, NX, NZ, 2, 16, HIDP), BF),
            pltpu.VMEM((32, 16, 128), BF),
            pltpu.VMEM((NT, 64, 256), BF),
            pltpu.VMEM((NT, 64, 256), BF),
            pltpu.VMEM((NP, 16, 128), BF),
            pltpu.VMEM((NP, 16, 128), BF),
            pltpu.VMEM((NG, 32, 128), BF),
            pltpu.VMEM((2, 32, 128), BF),
            pltpu.VMEM((NT, 64, 256), BF),
            pltpu.VMEM((256, D), BF),
            pltpu.VMEM((NP, 16, 384), BF),
            pltpu.VMEM((NP, 16, 384), BF),
            pltpu.VMEM((NG, 16, 384), BF),
            pltpu.VMEM((NP, 16, 256), BF),
            sem((7,)),
            sem, sem, sem((64,)), sem, sem,
            sem, sem, sem, sem((2,)),
            sem, sem, sem, sem,
            sem, sem,
            sem, sem((2, 2)), sem((2,)),
            sem, sem, sem, sem, sem, sem,
        ],
        compiler_params=pltpu.CompilerParams(
            collective_id=0, has_side_effects=True, vmem_limit_bytes=VLIM
        ),
    )(
        token_grads, hidden.reshape(2, 128, 512), proj_weight, proj_bias.reshape(1, 128),
        norm_gain.reshape(1, 512), down_weight.T, lengths,
    )
    return act, proj, gain.reshape(512), bias.reshape(128)


def solution(mesh):
    placed = (P("fsdp", None), P("fsdp", "tp"), P(None, "tp"), P(), P("tp"), P("tp", "fsdp"), P())
    return jax.shard_map(
        shards,
        mesh=mesh,
        in_specs=placed,
        out_specs=(P("fsdp", "tp"), P(None, "tp"), P("tp"), P()),
        check_vma=False,
    )
```

```python
import jax
import jax.numpy as jnp
from jax import lax
from jax.experimental import pallas as pl
from jax.experimental.pallas import tpu as pltpu
from jax.sharding import PartitionSpec as P

D = 2048
LEN = 512
NX, NZ, NG, NP, NT = 4, 8, 8, 16, 4
HIDL, HIDP = 1408, 1536
YREC, XREC = 28, {1: 29, 2: 30, 3: 31, 5: 56, 6: 57, 7: 58}
VLIM = 56 * 1024 * 1024
MESH = pl.DeviceIdType.MESH
HIGH = lax.Precision.HIGHEST
BF, F32, I32 = jnp.bfloat16, jnp.float32, jnp.int32
NT_DIMS = (((1,), (1,)), ((), ()))


def iota(shape, axis):
    return lax.broadcasted_iota(I32, shape, axis)


def split_hi_lo(value):
    hi = value.astype(BF).astype(F32)
    return hi, value - hi


def permute_rows(count, source_of, rows):
    hot = jnp.where(
        iota((count, count), 1) == source_of(iota((count, count), 0)), F32(1.0), F32(0.0)
    ).astype(BF)
    return jnp.dot(hot, rows, preferred_element_type=F32)


def kernel(
    tg_hbm, x_hbm, p_hbm, b_hbm, g_hbm, w_hbm, len_hbm,
    act_out, proj_out, gain_out, bias_out,
    act_ref, proj_ref, gain_ref, bias_ref, outs,
    tg_ref, xfull, p_ref, b_ref, g_ref, w_ref, len_ref,
    wfull, pgt, usend, urecv, s1src, s1dst, s2src, s2dst, dzfull, dhv, rs_src, rs_dst, zbuf, ag,
    ins, ringsend, sidesend, wr, sibs, sibr,
    s1ss, s1rs, s2ss, s2rs, us, ur, ps, pr, ds, dr, dhs, dhr, dfr, rss, rsr, zss, zsr, ags, agr,
):
    f = lax.axis_index("fsdp")
    t = lax.axis_index("tp")
    core = f % 2
    z = (f // 2) % NZ
    grp = f // 16
    xa = grp % NX
    yl = grp // NX
    p = f % 16

    def at_f(group, zpos, cpos):
        return group * 16 + zpos * 2 + cpos

    def peer_p(d):
        q = (p + d) % NP
        return q, grp * 16 + q

    def peer_g(d):
        q = (grp + d) % NG
        return q, q * 16 + p

    def peer_t(d):
        return (t + d) % NT

    def copy(src, dst, ssem, rsem, dev):
        return pltpu.make_async_remote_copy(
            src_ref=src, dst_ref=dst, send_sem=ssem, recv_sem=rsem,
            device_id=dev, device_id_type=MESH,
        )

    def each(lo, hi, body):
        for d in range(lo, hi):
            body(d)

    near_p = {"fsdp": peer_p(1)[1]}
    near_g = {"fsdp": peer_g(1)[1]}

    bar = pltpu.get_barrier_semaphore()

    def greet(dev):
        pl.semaphore_signal(bar, inc=1, device_id=dev, device_id_type=MESH)

    each(1, NP, lambda d: greet({"fsdp": peer_p(d)[1]}))
    each(1, NG, lambda d: greet({"fsdp": peer_g(d)[1]}))
    each(1, NT, lambda d: greet({"tp": peer_t(d)}))

    loads = [
        pltpu.make_async_copy(src, dst, ins.at[i])
        for i, (src, dst) in enumerate((
            (w_hbm, w_ref), (tg_hbm, tg_ref), (x_hbm, xfull.at[t]), (p_hbm, p_ref),
            (g_hbm, g_ref), (b_hbm, b_ref), (len_hbm, len_ref),
        ))
    ]
    for load in loads:
        load.start()

    loads[0].wait()
    wfull[yl, xa, z, core, :, 0:HIDL] = w_ref[...].astype(BF)
    loads[1].wait()
    carries = grp // 2 == t

    @pl.when(carries)
    def _():
        rows = permute_rows(
            256, lambda r: ((r >> 1) & 7) * 32 + (r >> 4) * 2 + (r & 1), tg_ref[...].astype(BF)
        )
        s1src[...] = rows.astype(BF).reshape(16, 16, 128)

    for load in loads[2:]:
        load.wait()
    gain = g_ref[...]
    pg = p_ref[...] * gain
    pg_hi = pg.astype(BF)
    pg_lo = (pg - pg_hi.astype(F32)).astype(BF)
    pgt[...] = pg.T.astype(BF).reshape(32, 16, 128)
    pl.semaphore_wait(bar, (NP - 1) + (NG - 1) + (NT - 1))

    def go(make):
        make().start()

    def sibling(piece):
        copy(piece, piece, sibs, sibr, {"fsdp": f + 1 - 2 * core}).start()

    own = wfull.at[yl, xa, z, core]
    met = wfull.at[1 - yl, xa, z, core]
    met_w = wfull.at[1 - yl, xa, z, core, :, pl.ds(0, HIDL)]
    met_p = wfull.at[1 - yl, xa, z, core, :, pl.ds(HIDL, 128)]
    own_w = wfull.at[yl, xa, z, core, :, pl.ds(0, HIDL)]
    own_p = wfull.at[yl, xa, z, core, :, pl.ds(HIDL, 128)]
    zdev = ({"fsdp": at_f(grp, (z + 1) % NZ, core)}, {"fsdp": at_f(grp, (z + NZ - 1) % NZ, core)})
    xdev = (
        {"fsdp": at_f(yl * NX + (xa + 1) % NX, z, core)},
        {"fsdp": at_f(yl * NX + (xa + NX - 1) % NX, z, core)},
    )

    ydev = {"fsdp": at_f((grp + NX) % NG, z, core)}

    def zslot(direction, s):
        return (z + NZ - s) % NZ if direction == 0 else (z + s) % NZ

    def piece0(i, zj):
        return wfull.at[yl if i < NX else 1 - yl, (xa + i % NX) % NX, zj, 0]

    def xdev_at(d):
        return {"fsdp": at_f(yl * NX + (xa + d) % NX, z, core)}

    def zmove0(direction, s, i):
        def make():
            piece = piece0(i, zslot(direction, s))
            return copy(piece, piece, ringsend, wr.at[direction * 32 + s * 8 + i], zdev[direction])

        return make

    def launch0(i):
        for direction in (0, 1):
            go(zmove0(direction, 0, i))
        sibling(piece0(i, z))

    def begin0(part, yrec):
        go(lambda: copy(part, part, sidesend, wr.at[yrec], ydev))
        for d in range(1, NX):
            go(lambda d=d: copy(part, part, sidesend, wr.at[XREC[d]], xdev_at(NX - d)))
        for direction in (0, 1):
            go(lambda: copy(part, part, ringsend, wr.at[direction * 32], zdev[direction]))

    def end_begin0():
        begin0(own_p, YREC - 1)
        sibling(own)

    def relay0(part, yrec):
        copy(part, part, sidesend, wr.at[yrec], ydev).wait_recv()
        for d in range(1, NX):
            go(lambda d=d: copy(part, part, sidesend, wr.at[XREC[NX + d]], xdev_at(NX - d)))
        for direction in (0, 1):
            go(lambda: copy(part, part, ringsend, wr.at[direction * 32 + NX], zdev[direction]))

    def end_relay0():
        relay0(met_p, YREC - 1)
        sibling(met)

    def ring0(i):
        def run():
            copy(own, own, sidesend, wr.at[XREC[i]], zdev[0]).wait_recv()
            launch0(i)

        return run

    def arrive0(s, direction, i):
        zmove0(direction, s - 1, i)().wait_recv()
        if s < 3 or (s == 3 and (i < 3) == (direction == 0)):
            go(zmove0(direction, s, i))
        sibling(piece0(i, zslot(direction, s)))

    def step0(s, i):
        def run():
            if s < 4 or i < 3:
                arrive0(s, 0, i)
            if s < 4 or i >= 3:
                arrive0(s, 1, i)

        return run

    todo0 = [lambda: begin0(own_w, YREC), end_begin0, lambda: relay0(met_w, YREC)]
    todo0 += [ring0(1), ring0(3), ring0(2), end_relay0, step0(1, 0), ring0(5), ring0(7), ring0(6)]
    order = (1, 3, 2, 4, 5, 7, 6)
    todo0 += [step0(1, i) for i in order]
    todo0 += [step0(2, i) for i in (0,) + order] + [step0(3, i) for i in (0,) + order]
    todo0 += [step0(4, i) for i in (0,) + order]

    hops = [(0, 0), (0, 1), (1, 1), (0, 2), (1, 2), (0, 3), (1, 3), (0, 4)]

    def piece1(xj, zj):
        return wfull.at[:, xj, zj, 1]

    def zmove1(direction, s):
        def make():
            piece = piece1(xa, zslot(direction, s))
            return copy(piece, piece, ringsend, wr.at[direction * 4 + s], zdev[direction])

        return make

    def xmove(direction, k):
        def make():
            piece = piece1(xa, zslot(*hops[k]))
            return copy(piece, piece, sidesend, wr.at[8 + direction * 8 + k], xdev[direction])

        return make

    def xforward(k):
        direction = k % 2

        def make():
            xj = (xa + NX - 1) % NX if direction == 0 else (xa + 1) % NX
            piece = piece1(xj, zslot(*hops[k]))
            return copy(piece, piece, sidesend, wr.at[24 + k], xdev[direction])

        return make

    def begin1(part):
        go(lambda: copy(part, part, ringsend, wr.at[32], ydev))

    def spread(k):
        go(xmove(0, k))
        go(xmove(1, k))
        sibling(piece1(xa, zslot(*hops[k])))

    def first1():
        copy(met, met, ringsend, wr.at[32], ydev).wait_recv()
        go(zmove1(0, 0))
        go(zmove1(1, 0))
        spread(0)

    def zstep1(k):
        def run():
            direction, s = hops[k]
            zmove1(direction, s - 1)().wait_recv()
            if s < 3 or (s == 3 and direction == 0):
                go(zmove1(direction, s))
            spread(k)

        return run

    def xstep1(k, direction):
        def run():
            xmove(direction, k)().wait_recv()
            xj = (xa + NX - 1) % NX if direction == 0 else (xa + 1) % NX
            if k % 2 == direction:
                go(xforward(k))
            sibling(piece1(xj, zslot(*hops[k])))

        return run

    def fstep1(k):
        def run():
            xforward(k)().wait_recv()
            sibling(piece1((xa + 2) % NX, zslot(*hops[k])))

        return run

    todo1 = [lambda: begin1(own_w), lambda: begin1(own_p), first1]
    for k in range(1, 8):
        todo1.append(zstep1(k))
        if k >= 3:
            todo1 += [xstep1(k - 3, 0), xstep1(k - 3, 1)]
        if k >= 6:
            todo1.append(fstep1(k - 6))
    for k in (5, 6, 7):
        todo1 += [xstep1(k, 0), xstep1(k, 1), fstep1(k - 3)]
    todo1 += [fstep1(k) for k in (5, 6, 7)]

    def advance(n0, n1):
        head0, head1 = todo0[:n0], todo1[:n1]
        del todo0[:n0], todo1[:n1]
        if head0:
            @pl.when(core == 0)
            def _():
                for run in head0:
                    run()
        if head1:
            @pl.when(core == 1)
            def _():
                for run in head1:
                    run()

    p_slab = f // 32
    p_row = f % 32
    p_src = pgt.at[p_row]

    @pl.when(p_slab == t)
    def _():
        def send(d):
            copy(p_src, own_p, ps, pr, {"tp": peer_t(d)}).start()

        each(1, NT, send)
        wfull[yl, xa, z, core, :, HIDL:HIDP] = pgt[p_row]

    @pl.when(carries)
    def _():
        def send(d):
            q, dev = peer_p(d)
            copy(s1src.at[q], s1dst.at[p], s1ss, s1rs, {"fsdp": dev}).start()

        each(1, NP, send)
        s1dst[p] = s1src[p]

    advance(1, 1)

    xv = xfull[t].reshape(256, 512)
    pu = lax.dot_general(xv, pg_hi, NT_DIMS, preferred_element_type=F32)
    pu = pu + lax.dot_general(xv, pg_lo, NT_DIMS, preferred_element_type=F32)
    xv = xv.astype(F32)
    sq_hi, sq_lo = split_hi_lo(jnp.sum(xv * xv, axis=1, keepdims=True))
    sq2 = jnp.where(iota((256, 128), 1) < 64, sq_hi, sq_lo)
    usend[:, :, 0:128] = pu.astype(BF).reshape(4, 64, 128)
    usend[:, :, 128:256] = sq2.astype(BF).reshape(4, 64, 128)

    def send_u(d):
        q = peer_t(d)
        copy(usend.at[q], urecv.at[t], us, ur, {"tp": q}).start()

    each(1, NT, send_u)
    urecv[t] = usend[t]

    tdev = ({"tp": (t + 1) % NT}, {"tp": (t + NT - 1) % NT})

    def x_move(direction, h):
        part = xfull.at[t, h]
        return copy(part, part, dhs, dhr.at[direction, h], tdev[direction])

    def x_forward(direction):
        part = xfull.at[(t + NT - 1) % NT if direction == 0 else (t + 1) % NT, direction]
        return copy(part, part, dhs, dfr.at[direction], tdev[direction])

    @pl.when(p_slab != t)
    def _():
        copy(p_src, own_p, ps, pr, tdev[0]).wait_recv()

    advance(2, 1)

    slot = grp % 2

    @pl.when(carries)
    def _():
        copy(s1src.at[0:15], s1dst.at[0:15], s1ss, s1rs, near_p).wait_recv()
        rows = permute_rows(
            256,
            lambda r: ((r >> 1) & 15) * 16 + (r >> 5) * 2 + (r & 1),
            s1dst[...].reshape(256, 128),
        )
        s2src[...] = rows.astype(BF).reshape(8, 32, 128)

        def send(d):
            q, dev = peer_g(d)
            copy(s2src.at[q], s2dst.at[slot], s2ss, s2rs.at[slot], {"fsdp": dev}).start()

        each(1, NG, send)
        s2dst[slot] = s2src[grp]

    advance(4, 1)

    copy(usend.at[0:3], urecv.at[0:3], us, ur, tdev[0]).wait_recv()
    summed = jnp.sum(urecv[...].astype(F32), axis=0)
    u = summed[:, 0:128]
    lane = iota((64, 128), 1)
    sq = jnp.sum(
        jnp.where((lane == 0) | (lane == 64), summed[:, 128:256], 0.0), axis=1, keepdims=True
    )
    inv = lax.rsqrt(sq / D + 1e-06)
    zvals = inv * u + b_ref[...]
    kinv = lax.rsqrt(jnp.sum(zvals * zvals, axis=1, keepdims=True) + 1e-06)
    emb = zvals * kinv
    advance(0, 1)

    for i in range(2):
        @pl.when(jnp.logical_not(carries & (slot == i)))
        def _(i=i):
            copy(s2src.at[0], s2dst.at[i], s2ss, s2rs.at[i], {"fsdp": peer_g(1)[1]}).wait_recv()

    position = core * 256 + t * 64 + iota((64, 128), 0)
    grads = jnp.where(
        position < len_ref[f // 2], s2dst[...].reshape(64, 128).astype(F32), 0.0
    )
    dz = kinv * (grads - emb * jnp.sum(emb * grads, axis=1, keepdims=True))
    cvals = jnp.sum(dz * u, axis=1, keepdims=True)
    coef = inv * inv * inv * cvals / D
    inv_hi, inv_lo = split_hi_lo(inv)
    coef_hi, coef_lo = split_hi_lo(coef)
    tail = jnp.where(
        lane < 64,
        jnp.where(lane < 32, inv_hi, inv_lo),
        jnp.where(lane < 96, coef_hi, coef_lo),
    )
    dzfull[t, :, 0:128] = dz.astype(BF)
    dzfull[t, :, 128:256] = tail.astype(BF)

    def send_dz(d):
        part = dzfull.at[t]
        copy(part, part, ds, dr, {"tp": peer_t(d)}).start()

    each(1, NT, send_dz)
    for direction in (0, 1):
        x_move(direction, direction).start()
    advance(8, 3)

    copy(dzfull.at[0:3], dzfull.at[0:3], ds, dr, tdev[0]).wait_recv()
    for direction in (0, 1):
        x_move(direction, 1 - direction).start()
    dzall = dzfull[:, :, 0:128].reshape(256, 128)
    tails = dzfull[:, :, 128:256].reshape(256, 128).astype(F32)
    lane = iota((256, 128), 1)
    inv = jnp.sum(jnp.where((lane == 0) | (lane == 32), tails, 0.0), axis=1, keepdims=True)
    coef = jnp.sum(jnp.where((lane == 64) | (lane == 96), tails, 0.0), axis=1, keepdims=True)
    dzf = dzall.astype(F32)
    xinv = (xfull[t].reshape(256, 512).astype(F32) * (inv * (1.0 / 64.0))).astype(BF)
    sums = jnp.dot(dzf.T.astype(BF), xinv, preferred_element_type=F32)
    bsum = jnp.sum(dzf, axis=0, keepdims=True) * (1.0 / 64.0)
    row8 = iota((8, 128), 0)
    extra = jnp.where(row8 == 0, bsum, 0.0)

    def pack_extra(value):
        hi, lo = split_hi_lo(value)
        return jnp.concatenate([hi, lo], axis=0).astype(BF)

    main = jnp.concatenate(
        [sums[:, 0:256].reshape(16, 8, 256), sums[:, 256:512].reshape(16, 8, 256)], axis=1
    )
    rs_src[:, :, 0:256] = main.astype(BF)
    rs_src[:, :, 256:384] = jnp.broadcast_to(pack_extra(extra)[None], (16, 16, 128))

    def send_rs(d):
        q, dev = peer_p(d)
        copy(rs_src.at[q], rs_dst.at[p], rss, rsr, {"fsdp": dev}).start()

    each(1, NP, send_rs)
    rs_dst[p] = rs_src[p]
    advance(10, 9)

    copy(rs_src.at[0:15], rs_dst.at[0:15], rss, rsr, near_p).wait_recv()
    part = jnp.sum(rs_dst[...].astype(F32), axis=0)
    zbuf[grp, :, 0:256] = part[:, 0:256].astype(BF)
    zbuf[grp, :, 256:384] = pack_extra(part[0:8, 256:384] + part[8:16, 256:384])

    def send_z(d):
        q, dev = peer_g(d)
        copy(zbuf.at[grp], zbuf.at[grp], zss, zsr, {"fsdp": dev}).start()

    each(1, NG, send_z)
    for direction in (0, 1):
        x_move(direction, direction).wait_recv()
        x_forward(direction).start()
    advance(9, 13)
    copy(zbuf.at[0:7], zbuf.at[0:7], zss, zsr, near_g).wait_recv()
    part = jnp.sum(zbuf[...].astype(F32), axis=0)
    ag[p] = part[:, 0:256].astype(BF)
    bias_ref[...] = (part[0:8, 256:384] + part[8:16, 256:384])[0:1]

    def send_ag(d):
        q, dev = peer_p(d)
        copy(ag.at[p], ag.at[p], ags, agr, {"fsdp": dev}).start()

    each(1, NP, send_ag)
    advance(len(todo0), len(todo1))

    for direction in (0, 1):
        x_move(direction, 1 - direction).wait_recv()
        x_forward(direction).wait_recv()
    copy(wfull.at[:, :, :, core], wfull.at[:, :, :, 1 - core], sibs, sibr, {"fsdp": f + 1 - 2 * core}).wait()
    for j in range(NT):
        for k in range(2):
            pgt_part = wfull[j // 2, (j % 2) * 2 + k, :, :, :, HIDL:HIDP].reshape(256, 128)
            dn = lax.dot_general(dzall, pgt_part, NT_DIMS, preferred_element_type=F32)
            xpart = xfull[j, :, :, k * 256 : k * 256 + 256].reshape(256, 256).astype(F32)
            lo = j * 512 + k * 256
            dhv[:, lo : lo + 256] = (inv * dn - xpart * coef).astype(BF)
    stores = []

    def store(src, dst):
        move = pltpu.make_async_copy(src, dst, outs.at[len(stores)])
        move.start()
        stores.append(move)

    store(bias_ref, bias_out)
    for lo, hi in ((0, 512), (512, 1024), (1024, 1408)):
        act_ref[:, lo:hi] = jnp.dot(
            dhv[...], wfull[:, :, :, :, :, lo:hi].reshape(D, hi - lo), preferred_element_type=F32
        ).astype(BF)
        store(act_ref.at[:, lo:hi], act_out.at[:, lo:hi])

    copy(rs_src.at[0:15], rs_dst.at[0:15], rss, rsr, near_p).wait_send()
    copy(zbuf.at[0:7], zbuf.at[0:7], zss, zsr, near_g).wait_send()
    copy(usend.at[0:3], urecv.at[0:3], us, ur, tdev[0]).wait_send()
    copy(dzfull.at[0:3], dzfull.at[0:3], ds, dr, tdev[0]).wait_send()
    copy(xfull.at[0:3], xfull.at[0:3], dhs, dfr.at[0], tdev[0]).wait_send()

    @pl.when(p_slab == t)
    def _():
        copy(pgt.at[0:3], pgt.at[0:3], ps, pr, tdev[0]).wait_send()

    @pl.when(carries)
    def _():
        copy(s1src.at[0:15], s1dst.at[0:15], s1ss, s1rs, near_p).wait_send()
        copy(s2src.at[0:7], s2src.at[0:7], s2ss, s2rs.at[0], near_g).wait_send()

    def all_left(part, send_sem):
        copy(part, part, send_sem, wr.at[0], zdev[0]).wait_send()

    @pl.when(core == 0)
    def _():
        all_left(wfull.at[:, :, 0:7, 0], ringsend)
        all_left(wfull.at[0, 0, 0:7, 0], sidesend)

    @pl.when(core == 1)
    def _():
        all_left(wfull.at[0, 0:3, 0:5, 1], ringsend)
        all_left(wfull.at[:, 0:3, :, 1], sidesend)

    copy(ag.at[0:15], ag.at[0:15], ags, agr, near_p).wait()
    full = ag[...].astype(F32)
    full = jnp.concatenate(
        [full[:, 0:8].reshape(128, 256), full[:, 8:16].reshape(128, 256)], axis=1
    )
    proj_ref[...] = full * gain
    gain_ref[...] = jnp.sum(full * p_ref[...], axis=0, keepdims=True)
    store(proj_ref, proj_out)
    store(gain_ref, gain_out)

    for move in stores:
        move.wait()


def shards(token_grads, hidden, proj_weight, proj_bias, norm_gain, down_weight, lengths):
    sem = pltpu.SemaphoreType.DMA
    anywhere = pl.BlockSpec(memory_space=pl.ANY)
    results = (
        jax.ShapeDtypeStruct((256, HIDL), BF),
        jax.ShapeDtypeStruct((128, 512), F32),
        jax.ShapeDtypeStruct((1, 512), F32),
        jax.ShapeDtypeStruct((1, 128), F32),
    )
    act, proj, gain, bias = pl.pallas_call(
        kernel,
        out_shape=results,
        in_specs=[anywhere] * 7,
        out_specs=(anywhere,) * 4,
        scratch_shapes=[
            pltpu.VMEM((256, HIDL), BF),
            pltpu.VMEM((128, 512), F32),
            pltpu.VMEM((1, 512), F32),
            pltpu.VMEM((1, 128), F32),
            sem((6,)),
            pltpu.VMEM((256, 128), F32),
            pltpu.VMEM((NT, 2, 128, 512), BF),
            pltpu.VMEM((128, 512), F32),
            pltpu.VMEM((1, 128), F32),
            pltpu.VMEM((1, 512), F32),
            pltpu.VMEM((16, HIDL), F32),
            pltpu.SMEM((64,), I32),
            pltpu.VMEM((2, NX, NZ, 2, 16, HIDP), BF),
            pltpu.VMEM((32, 16, 128), BF),
            pltpu.VMEM((NT, 64, 256), BF),
            pltpu.VMEM((NT, 64, 256), BF),
            pltpu.VMEM((NP, 16, 128), BF),
            pltpu.VMEM((NP, 16, 128), BF),
            pltpu.VMEM((NG, 32, 128), BF),
            pltpu.VMEM((2, 32, 128), BF),
            pltpu.VMEM((NT, 64, 256), BF),
            pltpu.VMEM((256, D), BF),
            pltpu.VMEM((NP, 16, 384), BF),
            pltpu.VMEM((NP, 16, 384), BF),
            pltpu.VMEM((NG, 16, 384), BF),
            pltpu.VMEM((NP, 16, 256), BF),
            sem((7,)),
            sem, sem, sem((64,)), sem, sem,
            sem, sem, sem, sem((2,)),
            sem, sem, sem, sem,
            sem, sem,
            sem, sem((2, 2)), sem((2,)),
            sem, sem, sem, sem, sem, sem,
        ],
        compiler_params=pltpu.CompilerParams(
            collective_id=0, has_side_effects=True, vmem_limit_bytes=VLIM
        ),
    )(
        token_grads, hidden.reshape(2, 128, 512), proj_weight, proj_bias.reshape(1, 128),
        norm_gain.reshape(1, 512), down_weight.T, lengths,
    )
    return act, proj, gain.reshape(512), bias.reshape(128)


def solution(mesh):
    placed = (P("fsdp", None), P("fsdp", "tp"), P(None, "tp"), P(), P("tp"), P("tp", "fsdp"), P())
    return jax.shard_map(
        shards,
        mesh=mesh,
        in_specs=placed,
        out_specs=(P("fsdp", "tp"), P(None, "tp"), P("tp"), P()),
        check_vma=False,
    )
```
